32 devices in a mesh: parts: 2 (over x), dp: 2 (over core), fsdp: 8 (over z, y).
Axes of the slice: x: 2, y: 2, z: 4, core: 2. Of those that a mesh axis runs over, the one named last changes fastest.
Arguments:
- tokens: bfloat16 [16, 256, 8192], P(('parts', 'dp'), None, 'fsdp'), parts along dimension 0, may hold values from -6 to 6
- lengths: int32 [4, 4], P(('parts', 'dp')), parts along dimension 0, may hold values from 1 to 256, 640 in all within a row
- gate_weight: bfloat16 [8192, 14336], P(None, 'fsdp'), may hold values from -0.0625 to 0.0625
- hidden_grad: bfloat16 [16, 256, 14336], P(('parts', 'dp'), None, 'fsdp'), parts along dimension 0, may hold values from -6 to 6
- in_proj: bfloat16 [8192, 64], replicated, may hold values from -0.0625 to 0.0625
- out_proj: bfloat16 [14336, 64], P('fsdp'), may hold values from -0.046875 to 0.046875
- query_sketch: bfloat16 [1024, 4096], P('fsdp', 'dp'), may hold values from -0.1796875 to 0.1796875
Outputs:
- train_sketch: float32 [16, 4096], P(('parts', 'dp'), 'fsdp'), parts along dimension 0
- scores: float32 [16, 1024], P(('parts', 'dp'), 'fsdp'), parts along dimension 0
The draws below stay inside these ranges and needn't reach their ends.
There are 2 independent parts, one for each index of `parts`. The reference program is written for one: setup_inputs(seed, part) draws one part's arguments, and reference() takes and returns one part's arrays. A program takes and returns all parts, laid end to end along the dimension named above; an argument that names none is the same for every part. Nothing has to cross between parts.
Inputs may be any that keep to these rules, and one draw needn't show every extreme that they name: Each row of lengths holds the lengths of one dp index's 4 examples; every row sums to exactly 640 and its largest entry is 256.
All inputs are finite; a program needn't handle non-finite values.
Results may differ from the reference program's by a relative error of at most 0.0042.
Values may be sent and summed in bfloat16 or wider, within the bound.
No kernel may reach another device: no remote copies, remote signals or barrier semaphores. Data moves between devices by JAX's collectives and lax.ppermute only.
A program may use at most 128 MiB of HBM per device.

```python
import math
import jax
import jax.numpy as jnp
import numpy as np
from jax import lax

D = 8192
FF = 14336
RANK_IN = 64
RANK_OUT = 64
SEQ = 256
EX_DEV = 4
LIVE_DEV = 640
EXAMPLES = 8
QUERIES = 1024
N_DP = 2


def block_levels(own_key, shape, shards, least, largest):
    level = 1.0
    for dim, parts in shards:
        draws = jax.random.uniform(jax.random.fold_in(jax.random.fold_in(own_key, 6), dim), (parts,), jnp.float32, least / len(shards), largest / len(shards))
        level = level * jnp.repeat(jnp.exp(draws), shape[dim] // parts).reshape((-1,) + (1,) * (len(shape) - 1 - dim))
    return level


def split_up(count, total, reach, skew):
    portions = [(1 << 20) // math.isqrt(standing ** skew) + 1 for standing in range(2, count + 1)]
    rest, counts = total - reach - (count - 1), [1] * (count - 1)
    while rest > 0:
        movable = [i for i in range(count - 1) if counts[i] < reach]
        pool, remaining = sum([portions[i] for i in movable]), rest
        for i in movable:
            extra = min(reach - counts[i], max(1, remaining * portions[i] // pool), rest)
            counts[i] = counts[i] + extra
            rest = rest - extra
    return np.array([reach] + counts)


def uneven_parts(stream_key, number_of, total, bound, skew):
    if number_of == 2:
        one = jax.random.randint(stream_key, (), max(1, total - bound), min(bound, total - 1) + 1)
        return jnp.stack([one, total - one])
    sizes = jnp.asarray(split_up(number_of, total, bound, skew), jnp.int32)
    twos = (number_of - 1) // 2
    giver, taker = sizes[1:1 + 2 * twos:2], sizes[2:2 + 2 * twos:2]
    room = jnp.minimum(giver - 1, bound - taker)
    shifted = jax.random.randint(jax.random.fold_in(stream_key, 1), (twos,), 0, 1 << 20) % (room + 1)
    sizes = sizes.at[1:1 + 2 * twos:2].set(giver - shifted).at[2:2 + 2 * twos:2].set(taker + shifted)
    return sizes[jax.random.permutation(jax.random.fold_in(stream_key, 2), number_of)]


def bell_draw(rng, extent, scale, bound, shards=(), kind=jnp.bfloat16):
    gain = block_levels(rng, extent, shards, -0.22, 0.18) if shards else 1.0
    values = jax.random.normal(rng, extent, jnp.float32) * scale * gain
    return jnp.minimum(jnp.maximum(values, -bound), bound).astype(kind)


def setup_inputs(seed: int = 0, part: int = 0) -> dict:
    streams_of = jax.random.split(jax.random.key(seed), 8)
    part_keys = jax.random.split(jax.random.fold_in(streams_of[7], part), 8)
    return {
        "tokens": bell_draw(part_keys[0], (EXAMPLES, SEQ, D), 1.0, 6.0, ((0, 2), (2, 8))),
        "lengths": jax.vmap(lambda own: uneven_parts(own, EX_DEV, LIVE_DEV, SEQ, 2))(jax.random.split(part_keys[1], N_DP)).reshape((N_DP, EX_DEV)).astype(jnp.int32),
        "gate_weight": bell_draw(streams_of[2], (D, FF), D ** -0.5, 0.0625, ((1, 8),)),
        "hidden_grad": bell_draw(part_keys[3], (EXAMPLES, SEQ, FF), 1.0, 6.0, ((0, 2), (2, 8))),
        "in_proj": bell_draw(streams_of[4], (D, RANK_IN), D ** -0.5, 0.0625),
        "out_proj": bell_draw(streams_of[5], (FF, RANK_OUT), FF ** -0.5, 0.046875, ((0, 8),)),
        "query_sketch": bell_draw(streams_of[6], (QUERIES, RANK_IN * RANK_OUT), 0.03, 0.1796875, ((0, 8), (1, 2))),
    }


def reference(tokens, lengths, gate_weight, hidden_grad, in_proj, out_proj, query_sketch):
    flat_rows = tokens.reshape(EXAMPLES * SEQ, D)
    gate_pre = jnp.dot(flat_rows, gate_weight, preferred_element_type=jnp.float32)
    up_grad = (hidden_grad.reshape(EXAMPLES * SEQ, FF).astype(jnp.float32) * jax.nn.silu(gate_pre)).astype(jnp.bfloat16)
    left_proj = jnp.dot(flat_rows, in_proj, preferred_element_type=jnp.float32)
    right_proj = jnp.dot(up_grad, out_proj, preferred_element_type=jnp.float32)
    position = jnp.arange(SEQ, dtype=jnp.int32)
    live_mask = (position[None, :] < lengths.reshape(EXAMPLES)[:, None]).astype(jnp.float32)
    left_proj = left_proj.reshape(EXAMPLES, SEQ, RANK_IN) * live_mask[:, :, None]
    right_proj = right_proj.reshape(EXAMPLES, SEQ, RANK_OUT)
    sketch = jnp.einsum('esi,esj->eij', left_proj, right_proj, precision=lax.Precision.HIGHEST)
    train_sketch = (sketch * (1.0 / math.sqrt(SEQ))).reshape(EXAMPLES, RANK_IN * RANK_OUT)
    sketch_half = train_sketch.astype(jnp.bfloat16)
    scores = jnp.einsum('ek,qk->eq', sketch_half, query_sketch, preferred_element_type=jnp.float32)
    return (train_sketch, scores)
```

```python
import math

import jax
import jax.numpy as jnp
from jax import lax
from jax.sharding import PartitionSpec as P

LIVE = 640
CHUNKS = 2


def ring_order(size, folded):
    if folded:
        return list(range(0, size, 2)) + list(range(size - 1, 0, -2))
    return list(range(size))


def pack_matrix(lengths, seq_len, dtype):
    seq_lens = lengths.reshape(-1)
    ends = jnp.cumsum(seq_lens)
    rows = jnp.arange(LIVE, dtype=jnp.int32)
    example = jnp.sum((rows[:, None] >= ends[None, :]).astype(jnp.int32), axis=1)
    starts = ends - seq_lens
    owners = example[:, None] == jnp.arange(seq_lens.shape[0], dtype=jnp.int32)[None, :]
    start = jnp.sum(jnp.where(owners, starts[None, :], 0), axis=1)
    source = example * seq_len + rows - start
    slots = jnp.arange(seq_lens.shape[0] * seq_len, dtype=jnp.int32)
    return (source[:, None] == slots[None, :]).astype(dtype), owners


def on_device(order, tokens, lengths, gate_weight, hidden_grad, in_proj, out_proj, query_sketch):
    examples, seq_len, width = tokens.shape
    rank_in, rank_out = in_proj.shape[1], out_proj.shape[1]
    size = len(order)
    cw = [(order[i], order[(i + 1) % size]) for i in range(size)]
    ccw = [(d, s) for s, d in cw]
    place = [0] * size
    for i, d in enumerate(order):
        place[d] = i
    me = jnp.asarray(place, jnp.int32)[lax.axis_index("fsdp")]
    order_ids = jnp.asarray(order, jnp.int32)

    pick, owners = pack_matrix(lengths, seq_len, tokens.dtype)
    flat_rows = tokens.reshape(examples * seq_len, width)
    flat_grads = hidden_grad.reshape(examples * seq_len, -1)
    rows_of = LIVE // CHUNKS
    picks = [pick[c * rows_of : (c + 1) * rows_of] for c in range(CHUNKS)]
    queries = lax.all_gather(query_sketch, "dp", axis=1, tiled=True)

    own = [jnp.dot(p, flat_rows, preferred_element_type=jnp.float32).astype(tokens.dtype) for p in picks]
    gate = [None] * CHUNKS
    left = [None] * CHUNKS

    def absorb(c, block, step):
        source = order_ids[lax.rem(me - step + size, size)]
        weight = lax.dynamic_slice_in_dim(gate_weight, source * width, width, 0)
        proj = lax.dynamic_slice_in_dim(in_proj, source * width, width, 0)
        g = jnp.dot(block, weight, preferred_element_type=jnp.float32)
        l = jnp.dot(block, proj, preferred_element_type=jnp.float32)
        gate[c] = g if gate[c] is None else gate[c] + g
        left[c] = l if left[c] is None else left[c] + l

    right_going, left_going = list(own), list(own)
    for step in range(1, size // 2 + 1):
        last = step == size // 2
        new_right, new_left = list(right_going), list(left_going)
        for c in range(CHUNKS):
            if not last or c % 2 == 0:
                new_right[c] = lax.ppermute(right_going[c], "fsdp", cw)
            if not last or c % 2 == 1:
                new_left[c] = lax.ppermute(left_going[c], "fsdp", ccw)
        for c in range(CHUNKS):
            if step == 1:
                absorb(c, own[c], 0)
            else:
                absorb(c, right_going[c], step - 1)
                absorb(c, left_going[c], 1 - step)
        right_going, left_going = new_right, new_left
    grads = [jnp.dot(p, flat_grads, preferred_element_type=jnp.float32) for p in picks]
    for c in range(CHUNKS):
        absorb(c, (right_going if c % 2 == 0 else left_going)[c], size // 2)

    total = None
    for c in range(CHUNKS):
        up_grad = (grads[c] * jax.nn.silu(gate[c])).astype(jnp.bfloat16)
        right = jnp.dot(up_grad, out_proj, preferred_element_type=jnp.float32)
        owned = owners[c * rows_of : (c + 1) * rows_of]
        weighted = jnp.where(owned[:, :, None], right[:, None, :], 0.0)
        weighted = weighted.reshape(rows_of, examples * rank_out)
        part = jnp.einsum("ri,rk->ik", left[c], weighted, precision=lax.Precision.HIGHEST)
        total = part if total is None else total + part
    hop = 1
    while hop < size:
        total = total + lax.ppermute(total, "fsdp", [(i, i ^ hop) for i in range(size)])
        hop *= 2
    sketch = total.reshape(rank_in, examples, rank_out).transpose(1, 0, 2)
    sketch = (sketch * (1.0 / math.sqrt(seq_len))).reshape(examples, rank_in * rank_out)
    share = sketch.shape[1] // size
    own_cols = lax.dynamic_slice_in_dim(sketch, lax.axis_index("fsdp") * share, share, 1)
    scores = jnp.einsum(
        "ek,qk->eq", sketch.astype(jnp.bfloat16), queries, preferred_element_type=jnp.float32
    )
    return (own_cols, scores)


def solution(mesh):
    size = mesh.shape["fsdp"]
    order = ring_order(size, folded=mesh.shape["parts"] == 2)

    def per_device(*args):
        return on_device(order, *args)

    return jax.shard_map(
        per_device,
        mesh=mesh,
        in_specs=(
            P(("parts", "dp"), None, "fsdp"),
            P(("parts", "dp"), None),
            P(None, "fsdp"),
            P(("parts", "dp"), None, "fsdp"),
            P(),
            P("fsdp", None),
            P("fsdp", "dp"),
        ),
        out_specs=(P(("parts", "dp"), "fsdp"), P(("parts", "dp"), "fsdp")),
        check_vma=False,
    )
```

```python
import functools
import math

import jax
import jax.numpy as jnp
from jax import lax
from jax.experimental import pallas as pl
from jax.experimental.pallas import tpu as pltpu
from jax.sharding import PartitionSpec as P

LIVE = 640
VMEM = 48 << 20
NT = (((1,), (1,)), ((), ()))
TN = (((0,), (0,)), ((), ()))


def ring_order(size, folded):
    if folded:
        return list(range(0, size, 2)) + list(range(size - 1, 0, -2))
    return list(range(size))


def dot(a, b):
    return jnp.dot(a, b, preferred_element_type=jnp.float32)


def row_sources(lens, examples, seq_len):
    row = lax.broadcasted_iota(jnp.int32, (LIVE, 1), 0)
    slot, owner, start = row, jnp.zeros_like(row), jnp.int32(0)
    for e in range(1, examples):
        start = start + lens[0, e - 1]
        slot = jnp.where(row >= start, row - start + e * seq_len, slot)
        owner = jnp.where(row >= start, e, owner)
    return slot, owner


def pack_kernel(examples, seq_len, lens, x_ref, out_ref, pick):
    @pl.when(pl.program_id(0) == 0)
    def _():
        slot, _ = row_sources(lens, examples, seq_len)
        columns = lax.broadcasted_iota(jnp.int32, (LIVE, examples * seq_len), 1)
        pick[...] = jnp.where(columns == slot, 1.0, 0.0).astype(pick.dtype)

    out_ref[...] = dot(pick[...], x_ref[...]).astype(out_ref.dtype)


def pack(lengths, rows, examples, seq_len, first, count, tile):
    slots = rows.shape[0]
    return pl.pallas_call(
        functools.partial(pack_kernel, examples, seq_len),
        out_shape=jax.ShapeDtypeStruct((LIVE, count), rows.dtype),
        grid=(count // tile,),
        in_specs=[
            pl.BlockSpec(memory_space=pltpu.SMEM),
            pl.BlockSpec((slots, tile), lambda j: (0, first // tile + j)),
        ],
        out_specs=pl.BlockSpec((LIVE, tile), lambda j: (0, j)),
        scratch_shapes=[pltpu.VMEM((LIVE, slots), rows.dtype)],
        compiler_params=pltpu.CompilerParams(vmem_limit_bytes=VMEM),
        cost_estimate=pl.CostEstimate(
            flops=2 * LIVE * slots * count, bytes_accessed=2 * (slots + LIVE) * count, transcendentals=0
        ),
    )(lengths, rows)


def products(xs, weights, halves):
    total = None
    for k, weight in enumerate(weights):
        part = xs[k * halves].shape[1]
        for h in range(halves):
            term = dot(xs[k * halves + h][...], weight[h * part : (h + 1) * part, :])
            total = term if total is None else total + term
    return total


def projections(xs, projs, halves):
    total = None
    for k, proj in enumerate(projs):
        part = xs[k * halves].shape[1]
        for h in range(halves):
            term = lax.dot_general(
                xs[k * halves + h][...],
                proj[:, h * part : (h + 1) * part],
                NT,
                preferred_element_type=jnp.float32,
            )
            total = term if total is None else total + term
    return total


def absorb_kernel(blocks, halves, first, where, *refs):
    xs, refs = refs[: blocks * halves], refs[blocks * halves :]
    weights, projs, refs = refs[:blocks], refs[blocks : 2 * blocks], refs[2 * blocks :]
    if first:
        gate_out, left_out = refs
    else:
        gate_in, left_in, gate_out, left_out = refs
    gate = products(xs, weights, halves)
    gate_out[...] = gate if first else gate_in[...] + gate

    @pl.when(pl.program_id(0) == 0)
    def _():
        left = projections(xs, projs, halves)
        left_out[...] = left if first else left_in[...] + left


def block_specs(xs, weight, proj_t, steps, halves, tile):
    width = xs[0].shape[1] * halves
    pick_w = [pl.BlockSpec((width, tile), lambda j, w, k=k: (w[k], j)) for k in steps]
    pick_p = [pl.BlockSpec((proj_t.shape[0], width), lambda j, w, k=k: (0, w[k])) for k in steps]
    return [pl.BlockSpec(x.shape, lambda j, w: (0, 0)) for x in xs] + pick_w + pick_p


def absorb(where, xs, weight, proj_t, state, steps, halves, tile):
    hidden, rank = weight.shape[1], proj_t.shape[0]
    depth = xs[0].shape[1] * halves * len(steps)
    blocks = len(steps)
    gate_spec = pl.BlockSpec((LIVE, tile), lambda j, w: (0, j))
    left_spec = pl.BlockSpec((LIVE, rank), lambda j, w: (0, 0))
    specs = block_specs(xs, weight, proj_t, steps, halves, tile)
    args = [where, *xs, *[weight] * blocks, *[proj_t] * blocks]
    aliases = {}
    if state is not None:
        aliases = {len(args): 0, len(args) + 1: 1}
        specs = specs + [gate_spec, left_spec]
        args = args + list(state)
    return pl.pallas_call(
        functools.partial(absorb_kernel, blocks, halves, state is None),
        out_shape=[
            jax.ShapeDtypeStruct((LIVE, hidden), jnp.float32),
            jax.ShapeDtypeStruct((LIVE, rank), jnp.float32),
        ],
        grid_spec=pltpu.PrefetchScalarGridSpec(
            num_scalar_prefetch=1,
            grid=(hidden // tile,),
            in_specs=specs,
            out_specs=[gate_spec, left_spec],
        ),
        input_output_aliases=aliases,
        compiler_params=pltpu.CompilerParams(vmem_limit_bytes=VMEM),
        cost_estimate=pl.CostEstimate(
            flops=2 * LIVE * depth * (hidden + 256),
            bytes_accessed=2 * depth * (hidden + LIVE) + 8 * LIVE * hidden,
            transcendentals=0,
        ),
    )(*args)


def finish_kernel(examples, seq_len, halves, where, lens, *refs):
    xs, refs = refs[:halves], refs[halves:]
    weight, proj, gate_in, left_in, grads, out_t, sketch_out, right = refs
    step = pl.program_id(0)
    gate = gate_in[...] + products(xs, [weight], halves)
    up_grad = (grads[...].astype(jnp.float32) * jax.nn.silu(gate)).astype(jnp.bfloat16)
    term = lax.dot_general(up_grad, out_t[...], NT, preferred_element_type=jnp.float32)

    @pl.when(step == 0)
    def _():
        right[...] = term

    @pl.when(step > 0)
    def _():
        right[...] += term

    @pl.when(step == pl.num_programs(0) - 1)
    def _():
        left = left_in[...] + projections(xs, [proj], halves)
        _, owner = row_sources(lens, examples, seq_len)
        total = right[...]
        weighted = jnp.concatenate([jnp.where(owner == e, total, 0.0) for e in range(examples)], axis=1)
        sketch_out[...] = lax.dot_general(
            left * (1.0 / math.sqrt(seq_len)),
            weighted,
            TN,
            precision=lax.Precision.HIGHEST,
            preferred_element_type=jnp.float32,
        )


def finish(where, lengths, xs, weight, proj_t, state, grads, out_t, steps, halves, tile, examples, seq_len):
    hidden, rank_in, rank_out = weight.shape[1], proj_t.shape[0], out_t.shape[0]
    depth = xs[0].shape[1] * halves
    gate_spec = pl.BlockSpec((LIVE, tile), lambda j, w: (0, j))
    return pl.pallas_call(
        functools.partial(finish_kernel, examples, seq_len, halves),
        out_shape=jax.ShapeDtypeStruct((rank_in, examples * rank_out), jnp.float32),
        grid_spec=pltpu.PrefetchScalarGridSpec(
            num_scalar_prefetch=1,
            grid=(hidden // tile,),
            in_specs=[pl.BlockSpec(memory_space=pltpu.SMEM)]
            + block_specs(xs, weight, proj_t, steps, halves, tile)
            + [
                gate_spec,
                pl.BlockSpec((LIVE, rank_in), lambda j, w: (0, 0)),
                gate_spec,
                pl.BlockSpec((rank_out, tile), lambda j, w: (0, j)),
            ],
            out_specs=pl.BlockSpec((rank_in, examples * rank_out), lambda j, w: (0, 0)),
            scratch_shapes=[pltpu.VMEM((LIVE, rank_out), jnp.float32)],
        ),
        compiler_params=pltpu.CompilerParams(vmem_limit_bytes=VMEM),
        cost_estimate=pl.CostEstimate(
            flops=2 * LIVE * (depth + 256) * (hidden + 256),
            bytes_accessed=2 * depth * (hidden + LIVE) + 6 * LIVE * hidden,
            transcendentals=LIVE * hidden,
        ),
    )(where, lengths, *xs, weight, proj_t, *state, grads, out_t)


def on_device(order, tokens, lengths, gate_weight, hidden_grad, in_proj, out_proj, query_sketch):
    examples, seq_len, width = tokens.shape
    hidden = hidden_grad.shape[2]
    rank_in, rank_out = in_proj.shape[1], out_proj.shape[1]
    size = len(order)
    half = size // 2
    right_way = [(order[i], order[(i + 1) % size]) for i in range(size)]
    left_way = [(d, s) for s, d in right_way]
    table = [[0] * size for _ in range(size)]
    for i, d in enumerate(order):
        table[d] = [order[(i - step) % size] for step in range(size)]
    where = jnp.asarray(table, jnp.int32)[lax.axis_index("fsdp")]
    tile = 256 if hidden % 256 == 0 else hidden
    halves = 2
    part = width // halves

    flat_rows = tokens.reshape(examples * seq_len, width)
    flat_grads = hidden_grad.reshape(examples * seq_len, hidden)
    own = [pack(lengths, flat_rows, examples, seq_len, h * part, part, part) for h in range(halves)]
    proj_t, out_t = in_proj.T, out_proj.T

    going = {"r": list(own), "l": list(own)}
    state = None
    for step in range(1, half + 1):
        arrived = {"r": [None] * halves, "l": [None] * halves}
        for h in range(halves):
            if step < half or h == 0:
                arrived["r"][h] = lax.ppermute(going["r"][h], "fsdp", right_way)
            if step < half or h == 1:
                arrived["l"][h] = lax.ppermute(going["l"][h], "fsdp", left_way)
        if step == 1:
            state = absorb(where, own, gate_weight, proj_t, None, [0], halves, tile)
            grads = pack(lengths, flat_grads, examples, seq_len, 0, hidden, tile)
            other = lax.ppermute(query_sketch, "dp", [(0, 1), (1, 0)])
        else:
            xs = going["r"] + going["l"]
            steps = [step - 1, size - step + 1]
            state = absorb(where, xs, gate_weight, proj_t, state, steps, halves, tile)
        going = arrived
    xs = [going["r"][0], going["l"][1]]
    total = finish(
        where, lengths, xs, gate_weight, proj_t, state, grads, out_t, [half], halves, tile, examples, seq_len
    )
    hop = 1
    while hop < size:
        total = total + lax.ppermute(total, "fsdp", [(i, i ^ hop) for i in range(size)])
        hop *= 2
    sketch = total.reshape(rank_in, examples, rank_out).transpose(1, 0, 2)
    sketch = sketch.reshape(examples, rank_in * rank_out)
    share = sketch.shape[1] // size
    own_cols = lax.dynamic_slice_in_dim(sketch, lax.axis_index("fsdp") * share, share, 1)
    first = lax.axis_index("dp") == 0
    queries = jnp.concatenate(
        [jnp.where(first, query_sketch, other), jnp.where(first, other, query_sketch)], axis=1
    )
    scores = jnp.einsum(
        "ek,qk->eq", sketch.astype(jnp.bfloat16), queries, preferred_element_type=jnp.float32
    )
    return (own_cols, scores)


def solution(mesh):
    order = ring_order(mesh.shape["fsdp"], folded=mesh.shape["parts"] == 2)

    def per_device(*args):
        return on_device(order, *args)

    return jax.shard_map(
        per_device,
        mesh=mesh,
        in_specs=(
            P(("parts", "dp"), None, "fsdp"),
            P(("parts", "dp"), None),
            P(None, "fsdp"),
            P(("parts", "dp"), None, "fsdp"),
            P(),
            P("fsdp", None),
            P("fsdp", "dp"),
        ),
        out_specs=(P(("parts", "dp"), "fsdp"), P(("parts", "dp"), "fsdp")),
        check_vma=False,
    )
```

```python
import functools
import math

import jax
import jax.numpy as jnp
from jax import lax
from jax.experimental import pallas as pl
from jax.experimental.pallas import tpu as pltpu
from jax.sharding import PartitionSpec as P

LIVE = 640
SMALL = 12 << 20
LARGE = 38 << 20
NT = (((1,), (1,)), ((), ()))
TN = (((0,), (0,)), ((), ()))


def ring_order(size, folded):
    if folded:
        return list(range(0, size, 2)) + list(range(size - 1, 0, -2))
    return list(range(size))


def dot(a, b):
    return jnp.dot(a, b, preferred_element_type=jnp.float32)


def row_sources(lens, examples, seq_len):
    row = lax.broadcasted_iota(jnp.int32, (LIVE, 1), 0)
    slot, owner, start = row, jnp.zeros_like(row), jnp.int32(0)
    for e in range(1, examples):
        start = start + lens[0, e - 1]
        slot = jnp.where(row >= start, row - start + e * seq_len, slot)
        owner = jnp.where(row >= start, e, owner)
    return slot, owner


def pack_kernel(examples, seq_len, lens, x_ref, out_ref, pick):
    @pl.when(pl.program_id(0) == 0)
    def _():
        slot, _ = row_sources(lens, examples, seq_len)
        columns = lax.broadcasted_iota(jnp.int32, (LIVE, examples * seq_len), 1)
        pick[...] = jnp.where(columns == slot, 1.0, 0.0).astype(pick.dtype)

    out_ref[...] = dot(pick[...], x_ref[...]).astype(out_ref.dtype)


def pack(lengths, rows, examples, seq_len, first, count, tile):
    slots = rows.shape[0]
    return pl.pallas_call(
        functools.partial(pack_kernel, examples, seq_len),
        out_shape=jax.ShapeDtypeStruct((LIVE, count), rows.dtype),
        grid=(count // tile,),
        in_specs=[
            pl.BlockSpec(memory_space=pltpu.SMEM),
            pl.BlockSpec((slots, tile), lambda j: (0, first // tile + j)),
        ],
        out_specs=pl.BlockSpec((LIVE, tile), lambda j: (0, j)),
        scratch_shapes=[pltpu.VMEM((LIVE, slots), rows.dtype)],
        compiler_params=pltpu.CompilerParams(vmem_limit_bytes=LARGE),
        cost_estimate=pl.CostEstimate(
            flops=2 * LIVE * slots * count, bytes_accessed=2 * (slots + LIVE) * count, transcendentals=0
        ),
    )(lengths, rows)


def project(x, proj_t):
    return lax.dot_general(x, proj_t, NT, preferred_element_type=jnp.float32)


def absorb_kernel(parts, first, final, tile, where, *refs):
    count = len(parts)
    xs, (weight, proj_t), refs = refs[:count], refs[count : count + 2], refs[count + 2 :]
    if not first:
        (gate_in, left_in), refs = refs[:2], refs[2:]
    gate, left, *handed, held, sems = refs
    depth = xs[0].shape[1]

    def start_of(step, h):
        return pl.multiple_of(where[step] * (2 * depth) + h * depth, depth)

    copies = []
    for i, (step, h) in enumerate(parts):
        copies.append(pltpu.make_async_copy(weight.at[pl.ds(start_of(step, h), depth), :], held.at[i], sems.at[i]))
    if handed:
        rows = pl.ds(start_of(final, 0), 2 * depth)
        copies.append(pltpu.make_async_copy(weight.at[rows, :], handed[0], sems.at[count]))
    for copy in copies:
        copy.start()
    total = None if first else left_in[...]
    for x, (step, h) in zip(xs, parts, strict=True):
        term = project(x[...], proj_t[:, pl.ds(start_of(step, h), depth)])
        total = term if total is None else total + term
    left[...] = total
    for copy in copies[:count]:
        copy.wait()

    def one(j, carry):
        columns = pl.ds(pl.multiple_of(j * tile, tile), tile)
        total = None if first else gate_in[:, columns]
        for i, x in enumerate(xs):
            term = dot(x[...], held[i, :, columns])
            total = term if total is None else total + term
        gate[:, columns] = total
        return carry

    lax.fori_loop(0, held.shape[2] // tile, one, 0)
    for copy in copies[count:]:
        copy.wait()


def in_vmem(count):
    return [pl.BlockSpec(memory_space=pltpu.VMEM)] * count


def absorb(where, parts, xs, weight, proj_t, state, tile, final=None):
    hidden, rank = weight.shape[1], proj_t.shape[0]
    args = [where, *xs, weight, proj_t, *(state or ())]
    aliases = {} if state is None else {len(args) - 2: 0, len(args) - 1: 1}
    depth, count = xs[0].shape[1], len(xs)
    handed = [] if final is None else [jax.ShapeDtypeStruct((2 * depth, hidden), weight.dtype)]
    return pl.pallas_call(
        functools.partial(absorb_kernel, parts, state is None, final, tile),
        out_shape=[
            jax.ShapeDtypeStruct((LIVE, hidden), jnp.float32),
            jax.ShapeDtypeStruct((LIVE, rank), jnp.float32),
        ]
        + handed,
        in_specs=[pl.BlockSpec(memory_space=pltpu.SMEM)]
        + in_vmem(count)
        + [pl.BlockSpec(memory_space=pltpu.HBM)]
        + in_vmem(len(args) - 2 - count),
        out_specs=in_vmem(2 + len(handed)),
        input_output_aliases=aliases,
        scratch_shapes=[
            pltpu.VMEM((count, depth, hidden), weight.dtype),
            pltpu.SemaphoreType.DMA((count + 1,)),
        ],
        compiler_params=pltpu.CompilerParams(vmem_limit_bytes=LARGE),
        cost_estimate=pl.CostEstimate(
            flops=2 * LIVE * depth * count * (hidden + 256),
            bytes_accessed=2 * depth * count * (hidden + LIVE) + 8 * LIVE * hidden,
            transcendentals=0,
        ),
    )(*args)


def finish_kernel(examples, seq_len, step, tile, where, lens, *refs):
    xs, refs = refs[:2], refs[2:]
    weight, proj_t, gate_in, left_in, grads, out_t, sketch, block, right = refs
    depth = xs[0].shape[1]
    row = pl.multiple_of(where[step] * (2 * depth), 2 * depth)
    block[:, :depth] = xs[0][...]
    block[:, depth:] = xs[1][...]
    right[...] = jnp.zeros_like(right)

    def one(j, carry):
        columns = pl.ds(pl.multiple_of(j * tile, tile), tile)
        gate = gate_in[:, columns] + dot(block[...], weight[:, columns])
        up_grad = (grads[:, columns].astype(jnp.float32) * jax.nn.silu(gate)).astype(jnp.bfloat16)
        right[...] += project(up_grad, out_t[:, columns])
        return carry

    lax.fori_loop(0, weight.shape[1] // tile, one, 0)
    left = left_in[...] + project(block[...], proj_t[:, pl.ds(row, 2 * depth)])
    _, owner = row_sources(lens, examples, seq_len)
    total = right[...]
    weighted = jnp.concatenate([jnp.where(owner == e, total, 0.0) for e in range(examples)], axis=1)
    sketch[...] = lax.dot_general(
        left * (1.0 / math.sqrt(seq_len)),
        weighted,
        TN,
        precision=lax.Precision.HIGHEST,
        preferred_element_type=jnp.float32,
    )


def finish(where, lengths, xs, weight, proj_t, state, grads, out_t, step, tile, examples, seq_len):
    hidden, rank_in, rank_out = weight.shape[1], proj_t.shape[0], out_t.shape[0]
    depth = xs[0].shape[1] * 2
    return pl.pallas_call(
        functools.partial(finish_kernel, examples, seq_len, step, tile),
        out_shape=jax.ShapeDtypeStruct((rank_in, examples * rank_out), jnp.float32),
        in_specs=[pl.BlockSpec(memory_space=pltpu.SMEM)] * 2 + in_vmem(8),
        out_specs=pl.BlockSpec(memory_space=pltpu.VMEM),
        scratch_shapes=[
            pltpu.VMEM((LIVE, depth), jnp.bfloat16),
            pltpu.VMEM((LIVE, rank_out), jnp.float32),
        ],
        compiler_params=pltpu.CompilerParams(vmem_limit_bytes=SMALL),
        cost_estimate=pl.CostEstimate(
            flops=2 * LIVE * (depth + 256) * (hidden + 256),
            bytes_accessed=2 * depth * (hidden + LIVE) + 6 * LIVE * hidden,
            transcendentals=LIVE * hidden,
        ),
    )(where, lengths, *xs, weight, proj_t, *state, grads, out_t)


def on_device(order, tokens, lengths, gate_weight, hidden_grad, in_proj, out_proj, query_sketch):
    examples, seq_len, width = tokens.shape
    hidden = hidden_grad.shape[2]
    rank_in, rank_out = in_proj.shape[1], out_proj.shape[1]
    size = len(order)
    half = size // 2
    right_way = [(order[i], order[(i + 1) % size]) for i in range(size)]
    left_way = [(d, s) for s, d in right_way]
    table = [[0] * size for _ in range(size)]
    for i, d in enumerate(order):
        table[d] = [order[(i - step) % size] for step in range(size)]
    where = jnp.asarray(table, jnp.int32)[lax.axis_index("fsdp")]
    tile = hidden
    halves = 2
    part = width // halves

    flat_rows = tokens.reshape(examples * seq_len, width)
    flat_grads = hidden_grad.reshape(examples * seq_len, hidden)
    own = [pack(lengths, flat_rows, examples, seq_len, h * part, part, part) for h in range(halves)]
    proj_t, out_t = in_proj.T, out_proj.T

    right, left = list(own), list(own)
    state = None
    for step in range(1, half + 1):
        for h in range(halves):
            if step == 2 and h == 0:
                right[h], left[h], state, grads = lax.optimization_barrier((right[h], left[h], state, grads))
            elif step > 1:
                right[h], left[h], state = lax.optimization_barrier((right[h], left[h], state))
            xs = [right[h], left[h]]
            if step < half or h == 0:
                right[h] = lax.ppermute(right[h], "fsdp", right_way)
            if step < half or h == 1:
                left[h] = lax.ppermute(left[h], "fsdp", left_way)
            if step > 1:
                parts = [(step - 1, h), (size - step + 1, h)]
                final = half if step == half and h == halves - 1 else None
                state = absorb(where, parts, xs, gate_weight, proj_t, state, tile, final)
        if step == 1:
            state = absorb(where, [(0, 0), (0, 1)], own, gate_weight, proj_t, None, tile)
            grads = pack(lengths, flat_grads, examples, seq_len, 0, hidden, tile)
            other = lax.ppermute(query_sketch, "dp", [(0, 1), (1, 0)])
    xs = [right[0], left[1]]
    *state, last_weight = state
    total = finish(
        where, lengths, xs, last_weight, proj_t, state, grads, out_t, half, tile, examples, seq_len
    )
    hop = 1
    while hop < size:
        total = total + lax.ppermute(total, "fsdp", [(i, i ^ hop) for i in range(size)])
        hop *= 2
    sketch = total.reshape(rank_in, examples, rank_out).transpose(1, 0, 2)
    sketch = sketch.reshape(examples, rank_in * rank_out)
    share = sketch.shape[1] // size
    own_cols = lax.dynamic_slice_in_dim(sketch, lax.axis_index("fsdp") * share, share, 1)
    first = lax.axis_index("dp") == 0
    queries = jnp.concatenate(
        [jnp.where(first, query_sketch, other), jnp.where(first, other, query_sketch)], axis=1
    )
    scores = jnp.einsum(
        "ek,qk->eq", sketch.astype(jnp.bfloat16), queries, preferred_element_type=jnp.float32
    )
    return (own_cols, scores)


def solution(mesh):
    order = ring_order(mesh.shape["fsdp"], folded=mesh.shape["parts"] == 2)

    def per_device(*args):
        return on_device(order, *args)

    return jax.shard_map(
        per_device,
        mesh=mesh,
        in_specs=(
            P(("parts", "dp"), None, "fsdp"),
            P(("parts", "dp"), None),
            P(None, "fsdp"),
            P(("parts", "dp"), None, "fsdp"),
            P(),
            P("fsdp", None),
            P("fsdp", "dp"),
        ),
        out_specs=(P(("parts", "dp"), "fsdp"), P(("parts", "dp"), "fsdp")),
        check_vma=False,
    )
```

```python
import functools
import math

import jax
import jax.numpy as jnp
from jax import lax
from jax.experimental import pallas as pl
from jax.experimental.pallas import tpu as pltpu
from jax.sharding import PartitionSpec as P

LIVE = 640
CUT = 384
WHOLE = 60 << 20
SMALL = 12 << 20
LARGE = 38 << 20
NT = (((1,), (1,)), ((), ()))
TN = (((0,), (0,)), ((), ()))


def ring_order(size, folded):
    if folded:
        return list(range(0, size, 2)) + list(range(size - 1, 0, -2))
    return list(range(size))


def reduce_hops(size):
    rounds, hop = [], 1
    while hop < size:
        rounds.append((hop, 2 * hop, 3 * hop) if 2 * hop < size else (hop,))
        hop *= 4
    return rounds


def dot(a, b):
    return jnp.dot(a, b, preferred_element_type=jnp.float32)


def row_sources(lens, examples, seq_len):
    row = lax.broadcasted_iota(jnp.int32, (LIVE, 1), 0)
    slot, owner, start = row, jnp.zeros_like(row), jnp.int32(0)
    for e in range(1, examples):
        start = start + lens[0, e - 1]
        slot = jnp.where(row >= start, row - start + e * seq_len, slot)
        owner = jnp.where(row >= start, e, owner)
    return slot, owner


def pack_kernel(examples, seq_len, lens, x_ref, out_ref, pick):
    @pl.when(pl.program_id(0) == 0)
    def _():
        slot, _ = row_sources(lens, examples, seq_len)
        columns = lax.broadcasted_iota(jnp.int32, (LIVE, examples * seq_len), 1)
        pick[...] = jnp.where(columns == slot, 1.0, 0.0).astype(pick.dtype)

    out_ref[...] = dot(pick[...], x_ref[...]).astype(out_ref.dtype)


def pack(lengths, rows, examples, seq_len, first, count, tile):
    slots = rows.shape[0]
    return pl.pallas_call(
        functools.partial(pack_kernel, examples, seq_len),
        out_shape=jax.ShapeDtypeStruct((LIVE, count), rows.dtype),
        grid=(count // tile,),
        in_specs=[
            pl.BlockSpec(memory_space=pltpu.SMEM),
            pl.BlockSpec((slots, tile), lambda j: (0, first // tile + j)),
        ],
        out_specs=pl.BlockSpec((LIVE, tile), lambda j: (0, j)),
        scratch_shapes=[pltpu.VMEM((LIVE, slots), rows.dtype)],
        compiler_params=pltpu.CompilerParams(vmem_limit_bytes=LARGE),
        cost_estimate=pl.CostEstimate(
            flops=2 * LIVE * slots * count, bytes_accessed=2 * (slots + LIVE) * count, transcendentals=0
        ),
    )(lengths, rows)


def project(x, proj_t):
    return lax.dot_general(x, proj_t, NT, preferred_element_type=jnp.float32)


def open_kernel(examples, seq_len, reach, lens_in, x_in, *refs):
    outs, (lens, x, pick, sem) = refs[:-4], refs[-4:]
    count = len(outs)
    slots, width = x.shape
    depth, rows = width // count, LIVE // 2
    lens_copy = pltpu.make_async_copy(lens_in, lens, sem.at[count])
    lens_copy.start()
    loads = []
    for h in range(count):
        columns = slice(h * depth, (h + 1) * depth)
        loads.append(pltpu.make_async_copy(x_in.at[:, columns], x.at[:, columns], sem.at[h]))
        loads[h].start()
    lens_copy.wait()
    slot, _ = row_sources(lens, examples, seq_len)
    for m in range(2):
        columns = lax.broadcasted_iota(jnp.int32, (rows, reach), 1) + m * (slots - reach)
        pick[m] = jnp.where(columns == slot[m * rows : (m + 1) * rows], 1.0, 0.0).astype(pick.dtype)
    for h, out in enumerate(outs):
        loads[h].wait()
        for m in range(2):
            first = m * (slots - reach)
            part = dot(pick[m], x[first : first + reach, h * depth : (h + 1) * depth])
            out[m * rows : (m + 1) * rows, :] = part.astype(out.dtype)


def open_pack(lengths, rows, examples, seq_len, halves):
    slots, width = rows.shape
    reach = -(-(slots - LIVE // 2) // 128) * 128
    return pl.pallas_call(
        functools.partial(open_kernel, examples, seq_len, reach),
        out_shape=[jax.ShapeDtypeStruct((LIVE, width // halves), rows.dtype)] * halves,
        in_specs=[pl.BlockSpec(memory_space=pl.ANY)] * 2,
        out_specs=[pl.BlockSpec(memory_space=pltpu.VMEM)] * halves,
        scratch_shapes=[
            pltpu.SMEM(lengths.shape, lengths.dtype),
            pltpu.VMEM(rows.shape, rows.dtype),
            pltpu.VMEM((2, LIVE // 2, reach), rows.dtype),
            pltpu.SemaphoreType.DMA((halves + 1,)),
        ],
        compiler_params=pltpu.CompilerParams(vmem_limit_bytes=WHOLE),
        cost_estimate=pl.CostEstimate(
            flops=2 * LIVE * slots * width, bytes_accessed=2 * (slots + LIVE) * width, transcendentals=0
        ),
    )(lengths, rows)


def absorb_kernel(parts, first, final, tile, where, *refs):
    count = len(parts)
    xs, (weight, proj_t), refs = refs[:count], refs[count : count + 2], refs[count + 2 :]
    if not first:
        (gate_in, left_in), refs = refs[:2], refs[2:]
    gate, left, *handed, held, sems = refs
    depth = xs[0].shape[1]

    def start_of(step, h):
        return pl.multiple_of(where[step] * (2 * depth) + h * depth, depth)

    copies = []
    for i, (step, h) in enumerate(parts):
        copies.append(pltpu.make_async_copy(weight.at[pl.ds(start_of(step, h), depth), :], held.at[i], sems.at[i]))
    if handed:
        rows = pl.ds(start_of(final, 0), 2 * depth)
        copies.append(pltpu.make_async_copy(weight.at[rows, :], handed[0], sems.at[count]))
    for copy in copies:
        copy.start()
    total = None if first else left_in[...]
    for x, (step, h) in zip(xs, parts, strict=True):
        term = project(x[...], proj_t[:, pl.ds(start_of(step, h), depth)])
        total = term if total is None else total + term
    left[...] = total
    for copy in copies[:count]:
        copy.wait()

    def one(j, carry):
        columns = pl.ds(pl.multiple_of(j * tile, tile), tile)
        total = None if first else gate_in[:, columns]
        for i, x in enumerate(xs):
            term = dot(x[...], held[i, :, columns])
            total = term if total is None else total + term
        gate[:, columns] = total
        return carry

    lax.fori_loop(0, held.shape[2] // tile, one, 0)
    for copy in copies[count:]:
        copy.wait()


def in_vmem(count):
    return [pl.BlockSpec(memory_space=pltpu.VMEM)] * count


def absorb(where, parts, xs, weight, proj_t, state, tile, final=None):
    hidden, rank = weight.shape[1], proj_t.shape[0]
    args = [where, *xs, weight, proj_t, *(state or ())]
    aliases = {} if state is None else {len(args) - 2: 0, len(args) - 1: 1}
    depth, count = xs[0].shape[1], len(xs)
    handed = [] if final is None else [jax.ShapeDtypeStruct((2 * depth, hidden), weight.dtype)]
    return pl.pallas_call(
        functools.partial(absorb_kernel, parts, state is None, final, tile),
        out_shape=[
            jax.ShapeDtypeStruct((LIVE, hidden), jnp.float32),
            jax.ShapeDtypeStruct((LIVE, rank), jnp.float32),
        ]
        + handed,
        in_specs=[pl.BlockSpec(memory_space=pltpu.SMEM)]
        + in_vmem(count)
        + [pl.BlockSpec(memory_space=pltpu.HBM)]
        + in_vmem(len(args) - 2 - count),
        out_specs=in_vmem(2 + len(handed)),
        input_output_aliases=aliases,
        scratch_shapes=[
            pltpu.VMEM((count, depth, hidden), weight.dtype),
            pltpu.SemaphoreType.DMA((count + 1,)),
        ],
        compiler_params=pltpu.CompilerParams(vmem_limit_bytes=LARGE),
        cost_estimate=pl.CostEstimate(
            flops=2 * LIVE * depth * count * (hidden + 256),
            bytes_accessed=2 * depth * count * (hidden + LIVE) + 8 * LIVE * hidden,
            transcendentals=0,
        ),
    )(*args)


def finish_kernel(examples, seq_len, step, first, where, lens, *refs):
    xs, refs = refs[:2], refs[2:]
    weight, proj_t, gate_in, left_in, grads, out_t, *before, sketch, block = refs
    count, depth = xs[0].shape
    rows = slice(first, first + count)
    row = pl.multiple_of(where[step] * (2 * depth), 2 * depth)
    block[:, :depth] = xs[0][...]
    block[:, depth:] = xs[1][...]
    gate = gate_in[rows, :] + dot(block[...], weight[...])
    up_grad = (grads[rows, :].astype(jnp.float32) * jax.nn.silu(gate)).astype(jnp.bfloat16)
    right = project(up_grad, out_t[...])
    left = left_in[rows, :] + project(block[...], proj_t[:, pl.ds(row, 2 * depth)])
    _, owner = row_sources(lens, examples, seq_len)
    owner = owner[rows, :]
    weighted = jnp.concatenate([jnp.where(owner == e, right, 0.0) for e in range(examples)], axis=1)
    term = lax.dot_general(
        left * (1.0 / math.sqrt(seq_len)),
        weighted,
        TN,
        precision=lax.Precision.HIGHEST,
        preferred_element_type=jnp.float32,
    )
    sketch[...] = before[0][...] + term if before else term


def finish(where, lengths, xs, weight, proj_t, state, grads, out_t, before, step, first, examples, seq_len):
    hidden, rank_in, rank_out = weight.shape[1], proj_t.shape[0], out_t.shape[0]
    count, depth = xs[0].shape[0], xs[0].shape[1] * 2
    args = [*xs, weight, proj_t, *state, grads, out_t, *([] if before is None else [before])]
    return pl.pallas_call(
        functools.partial(finish_kernel, examples, seq_len, step, first),
        out_shape=jax.ShapeDtypeStruct((rank_in, examples * rank_out), jnp.float32),
        in_specs=[pl.BlockSpec(memory_space=pltpu.SMEM)] * 2 + in_vmem(len(args)),
        out_specs=pl.BlockSpec(memory_space=pltpu.VMEM),
        scratch_shapes=[pltpu.VMEM((count, depth), jnp.bfloat16)],
        compiler_params=pltpu.CompilerParams(vmem_limit_bytes=SMALL),
        cost_estimate=pl.CostEstimate(
            flops=2 * count * (depth + 256) * (hidden + 256),
            bytes_accessed=2 * depth * (hidden + count) + 6 * count * hidden,
            transcendentals=count * hidden,
        ),
    )(where, lengths, *args)


def on_device(order, tokens, lengths, gate_weight, hidden_grad, in_proj, out_proj, query_sketch):
    examples, seq_len, width = tokens.shape
    hidden = hidden_grad.shape[2]
    rank_in, rank_out = in_proj.shape[1], out_proj.shape[1]
    size = len(order)
    half = size // 2
    right_way = [(order[i], order[(i + 1) % size]) for i in range(size)]
    left_way = [(d, s) for s, d in right_way]
    table = [[0] * size for _ in range(size)]
    for i, d in enumerate(order):
        table[d] = [order[(i - step) % size] for step in range(size)]
    where = jnp.asarray(table, jnp.int32)[lax.axis_index("fsdp")]
    tile = hidden
    halves = 2

    flat_rows = tokens.reshape(examples * seq_len, width)
    flat_grads = hidden_grad.reshape(examples * seq_len, hidden)
    own = open_pack(lengths, flat_rows, examples, seq_len, halves)
    proj_t, out_t = in_proj.T, out_proj.T

    right, left = list(own), list(own)
    state = None
    for step in range(1, half):
        for h in range(halves):
            o = 1 - h
            if step == 2 and h == 0:
                right[h], left[o], state, grads = lax.optimization_barrier((right[h], left[o], state, grads))
            elif step > 1:
                right[h], left[o], state = lax.optimization_barrier((right[h], left[o], state))
            xs = [right[h], left[o]]
            right[h] = lax.ppermute(right[h], "fsdp", right_way)
            left[o] = lax.ppermute(left[o], "fsdp", left_way)
            if step > 1:
                parts = [(step - 1, h), (size - step + 1, o)]
                state = absorb(where, parts, xs, gate_weight, proj_t, state, tile)
        if step == 1:
            state = absorb(where, [(0, 0), (0, 1)], own, gate_weight, proj_t, None, tile)
            grads = pack(lengths, flat_grads, examples, seq_len, 0, hidden, tile)
            other = lax.ppermute(query_sketch, "dp", [(0, 1), (1, 0)])
    right[0], left[1], state = lax.optimization_barrier((right[0], left[1], state))
    cuts = [(0, CUT), (CUT, LIVE)]
    last = [
        [lax.ppermute(right[0][a:b], "fsdp", right_way), lax.ppermute(left[1][a:b], "fsdp", left_way)]
        for a, b in cuts
    ]
    for h in range(halves):
        parts = [(half - 1, h), (size - half + 1, 1 - h)]
        final = half if h == halves - 1 else None
        state = absorb(where, parts, [right[h], left[1 - h]], gate_weight, proj_t, state, tile, final)
    *state, last_weight = state
    total = None
    for xs, (a, _) in zip(last, cuts, strict=True):
        total = finish(
            where, lengths, xs, last_weight, proj_t, state, grads, out_t, total, half, a, examples, seq_len
        )
    for hops in reduce_hops(size):
        low = total.astype(jnp.bfloat16)
        for hop in hops:
            total = total + lax.ppermute(low, "fsdp", [(i, i ^ hop) for i in range(size)]).astype(jnp.float32)
    sketch = total.reshape(rank_in, examples, rank_out).transpose(1, 0, 2)
    sketch = sketch.reshape(examples, rank_in * rank_out)
    share = sketch.shape[1] // size
    own_cols = lax.dynamic_slice_in_dim(sketch, lax.axis_index("fsdp") * share, share, 1)
    first = lax.axis_index("dp") == 0
    queries = jnp.concatenate(
        [jnp.where(first, query_sketch, other), jnp.where(first, other, query_sketch)], axis=1
    )
    scores = jnp.einsum(
        "ek,qk->eq", sketch.astype(jnp.bfloat16), queries, preferred_element_type=jnp.float32
    )
    return (own_cols, scores)


def solution(mesh):
    order = ring_order(mesh.shape["fsdp"], folded=mesh.shape["parts"] == 2)

    def per_device(*args):
        return on_device(order, *args)

    return jax.shard_map(
        per_device,
        mesh=mesh,
        in_specs=(
            P(("parts", "dp"), None, "fsdp"),
            P(("parts", "dp"), None),
            P(None, "fsdp"),
            P(("parts", "dp"), None, "fsdp"),
            P(),
            P("fsdp", None),
            P("fsdp", "dp"),
        ),
        out_specs=(P(("parts", "dp"), "fsdp"), P(("parts", "dp"), "fsdp")),
        check_vma=False,
    )
```

```python
import functools
import math

import jax
import jax.numpy as jnp
from jax import lax
from jax.experimental import pallas as pl
from jax.experimental.pallas import tpu as pltpu
from jax.sharding import PartitionSpec as P

LIVE = 640
CUT = 384
WHOLE = 60 << 20
SMALL = 12 << 20
LARGE = 38 << 20
NT = (((1,), (1,)), ((), ()))
TN = (((0,), (0,)), ((), ()))


def ring_order(size, folded):
    if folded:
        return list(range(0, size, 2)) + list(range(size - 1, 0, -2))
    return list(range(size))


def reduce_hops(size):
    rounds, hop = [], 1
    while hop < size:
        rounds.append((hop, 2 * hop, 3 * hop) if 2 * hop < size else (hop,))
        hop *= 4
    return rounds


def dot(a, b):
    return jnp.dot(a, b, preferred_element_type=jnp.float32)


def row_sources(lens, examples, seq_len):
    row = lax.broadcasted_iota(jnp.int32, (LIVE, 1), 0)
    slot, owner, start = row, jnp.zeros_like(row), jnp.int32(0)
    for e in range(1, examples):
        start = start + lens[0, e - 1]
        slot = jnp.where(row >= start, row - start + e * seq_len, slot)
        owner = jnp.where(row >= start, e, owner)
    return slot, owner


def pack_kernel(examples, seq_len, lens, x_ref, out_ref, pick):
    @pl.when(pl.program_id(0) == 0)
    def _():
        slot, _ = row_sources(lens, examples, seq_len)
        columns = lax.broadcasted_iota(jnp.int32, (LIVE, examples * seq_len), 1)
        pick[...] = jnp.where(columns == slot, 1.0, 0.0).astype(pick.dtype)

    out_ref[...] = dot(pick[...], x_ref[...]).astype(out_ref.dtype)


def pack(lengths, rows, examples, seq_len, first, count, tile):
    slots = rows.shape[0]
    return pl.pallas_call(
        functools.partial(pack_kernel, examples, seq_len),
        out_shape=jax.ShapeDtypeStruct((LIVE, count), rows.dtype),
        grid=(count // tile,),
        in_specs=[
            pl.BlockSpec(memory_space=pltpu.SMEM),
            pl.BlockSpec((slots, tile), lambda j: (0, first // tile + j)),
        ],
        out_specs=pl.BlockSpec((LIVE, tile), lambda j: (0, j)),
        scratch_shapes=[pltpu.VMEM((LIVE, slots), rows.dtype)],
        compiler_params=pltpu.CompilerParams(vmem_limit_bytes=LARGE),
        cost_estimate=pl.CostEstimate(
            flops=2 * LIVE * slots * count, bytes_accessed=2 * (slots + LIVE) * count, transcendentals=0
        ),
    )(lengths, rows)


def project(x, proj_t):
    return lax.dot_general(x, proj_t, NT, preferred_element_type=jnp.float32)


def open_kernel(examples, seq_len, reach, lens_in, x_in, *refs):
    outs, (lens, x, pick, sem) = refs[:-4], refs[-4:]
    count = len(outs)
    slots, width = x.shape
    depth, rows = width // count, LIVE // 2
    lens_copy = pltpu.make_async_copy(lens_in, lens, sem.at[count])
    lens_copy.start()
    loads = []
    for h in range(count):
        columns = slice(h * depth, (h + 1) * depth)
        loads.append(pltpu.make_async_copy(x_in.at[:, columns], x.at[:, columns], sem.at[h]))
        loads[h].start()
    lens_copy.wait()
    slot, _ = row_sources(lens, examples, seq_len)
    for m in range(2):
        columns = lax.broadcasted_iota(jnp.int32, (rows, reach), 1) + m * (slots - reach)
        pick[m] = jnp.where(columns == slot[m * rows : (m + 1) * rows], 1.0, 0.0).astype(pick.dtype)
    for h, out in enumerate(outs):
        loads[h].wait()
        for m in range(2):
            first = m * (slots - reach)
            part = dot(pick[m], x[first : first + reach, h * depth : (h + 1) * depth])
            out[m * rows : (m + 1) * rows, :] = part.astype(out.dtype)


def open_pack(lengths, rows, examples, seq_len, halves):
    slots, width = rows.shape
    reach = -(-(slots - LIVE // 2) // 128) * 128
    return pl.pallas_call(
        functools.partial(open_kernel, examples, seq_len, reach),
        out_shape=[jax.ShapeDtypeStruct((LIVE, width // halves), rows.dtype)] * halves,
        in_specs=[pl.BlockSpec(memory_space=pl.ANY)] * 2,
        out_specs=[pl.BlockSpec(memory_space=pltpu.VMEM)] * halves,
        scratch_shapes=[
            pltpu.SMEM(lengths.shape, lengths.dtype),
            pltpu.VMEM(rows.shape, rows.dtype),
            pltpu.VMEM((2, LIVE // 2, reach), rows.dtype),
            pltpu.SemaphoreType.DMA((halves + 1,)),
        ],
        compiler_params=pltpu.CompilerParams(vmem_limit_bytes=WHOLE),
        cost_estimate=pl.CostEstimate(
            flops=2 * LIVE * slots * width, bytes_accessed=2 * (slots + LIVE) * width, transcendentals=0
        ),
    )(lengths, rows)


def absorb_kernel(parts, first, final, tile, where, *refs):
    count = len(parts)
    xs, (weight, proj_t), refs = refs[:count], refs[count : count + 2], refs[count + 2 :]
    if not first:
        (gate_in, left_in), refs = refs[:2], refs[2:]
    gate, left, *handed, held, sems = refs
    depth = xs[0].shape[1]

    def start_of(step, h):
        return pl.multiple_of(where[step] * (2 * depth) + h * depth, depth)

    copies = []
    for i, (step, h) in enumerate(parts):
        copies.append(pltpu.make_async_copy(weight.at[pl.ds(start_of(step, h), depth), :], held.at[i], sems.at[i]))
    if handed:
        rows = pl.ds(start_of(final, 0), 2 * depth)
        copies.append(pltpu.make_async_copy(weight.at[rows, :], handed[0], sems.at[count]))
    for copy in copies:
        copy.start()
    total = None if first else left_in[...]
    for x, (step, h) in zip(xs, parts, strict=True):
        term = project(x[...], proj_t[:, pl.ds(start_of(step, h), depth)])
        total = term if total is None else total + term
    left[...] = total
    for copy in copies[:count]:
        copy.wait()

    def one(j, carry):
        columns = pl.ds(pl.multiple_of(j * tile, tile), tile)
        total = None if first else gate_in[:, columns]
        for i, x in enumerate(xs):
            term = dot(x[...], held[i, :, columns])
            total = term if total is None else total + term
        gate[:, columns] = total
        return carry

    lax.fori_loop(0, held.shape[2] // tile, one, 0)
    for copy in copies[count:]:
        copy.wait()


def in_vmem(count):
    return [pl.BlockSpec(memory_space=pltpu.VMEM)] * count


def absorb(where, parts, xs, weight, proj_t, state, tile, final=None):
    hidden, rank = weight.shape[1], proj_t.shape[0]
    args = [where, *xs, weight, proj_t, *(state or ())]
    aliases = {} if state is None else {len(args) - 2: 0, len(args) - 1: 1}
    depth, count = xs[0].shape[1], len(xs)
    handed = [] if final is None else [jax.ShapeDtypeStruct((2 * depth, hidden), weight.dtype)]
    return pl.pallas_call(
        functools.partial(absorb_kernel, parts, state is None, final, tile),
        out_shape=[
            jax.ShapeDtypeStruct((LIVE, hidden), jnp.float32),
            jax.ShapeDtypeStruct((LIVE, rank), jnp.float32),
        ]
        + handed,
        in_specs=[pl.BlockSpec(memory_space=pltpu.SMEM)]
        + in_vmem(count)
        + [pl.BlockSpec(memory_space=pltpu.HBM)]
        + in_vmem(len(args) - 2 - count),
        out_specs=in_vmem(2 + len(handed)),
        input_output_aliases=aliases,
        scratch_shapes=[
            pltpu.VMEM((count, depth, hidden), weight.dtype),
            pltpu.SemaphoreType.DMA((count + 1,)),
        ],
        compiler_params=pltpu.CompilerParams(vmem_limit_bytes=LARGE),
        cost_estimate=pl.CostEstimate(
            flops=2 * LIVE * depth * count * (hidden + 256),
            bytes_accessed=2 * depth * count * (hidden + LIVE) + 8 * LIVE * hidden,
            transcendentals=0,
        ),
    )(*args)


def finish_kernel(examples, seq_len, step, first, where, lens, *refs):
    xs, refs = refs[:2], refs[2:]
    weight, proj_t, gate_in, left_in, grads, out_t, *before, sketch, block = refs
    count, depth = xs[0].shape
    rows = slice(first, first + count)
    row = pl.multiple_of(where[step] * (2 * depth), 2 * depth)
    block[:, :depth] = xs[0][...]
    block[:, depth:] = xs[1][...]
    gate = gate_in[rows, :] + dot(block[...], weight[...])
    up_grad = (grads[rows, :].astype(jnp.float32) * jax.nn.silu(gate)).astype(jnp.bfloat16)
    right = project(up_grad, out_t[...])
    left = left_in[rows, :] + project(block[...], proj_t[:, pl.ds(row, 2 * depth)])
    _, owner = row_sources(lens, examples, seq_len)
    owner = owner[rows, :]
    weighted = jnp.concatenate([jnp.where(owner == e, right, 0.0) for e in range(examples)], axis=1)
    term = lax.dot_general(
        left * (1.0 / math.sqrt(seq_len)),
        weighted,
        TN,
        precision=lax.Precision.HIGHEST,
        preferred_element_type=jnp.float32,
    )
    sketch[...] = before[0][...] + term if before else term


def finish(where, lengths, xs, weight, proj_t, state, grads, out_t, before, step, first, examples, seq_len):
    hidden, rank_in, rank_out = weight.shape[1], proj_t.shape[0], out_t.shape[0]
    count, depth = xs[0].shape[0], xs[0].shape[1] * 2
    args = [*xs, weight, proj_t, *state, grads, out_t, *([] if before is None else [before])]
    return pl.pallas_call(
        functools.partial(finish_kernel, examples, seq_len, step, first),
        out_shape=jax.ShapeDtypeStruct((rank_in, examples * rank_out), jnp.float32),
        in_specs=[pl.BlockSpec(memory_space=pltpu.SMEM)] * 2 + in_vmem(len(args)),
        out_specs=pl.BlockSpec(memory_space=pltpu.VMEM),
        scratch_shapes=[pltpu.VMEM((count, depth), jnp.bfloat16)],
        compiler_params=pltpu.CompilerParams(vmem_limit_bytes=SMALL),
        cost_estimate=pl.CostEstimate(
            flops=2 * count * (depth + 256) * (hidden + 256),
            bytes_accessed=2 * depth * (hidden + count) + 6 * count * hidden,
            transcendentals=count * hidden,
        ),
    )(where, lengths, *args)


def on_device(order, tokens, lengths, gate_weight, hidden_grad, in_proj, out_proj, query_sketch):
    examples, seq_len, width = tokens.shape
    hidden = hidden_grad.shape[2]
    rank_in, rank_out = in_proj.shape[1], out_proj.shape[1]
    size = len(order)
    half = size // 2
    right_way = [(order[i], order[(i + 1) % size]) for i in range(size)]
    left_way = [(d, s) for s, d in right_way]
    table = [[0] * size for _ in range(size)]
    for i, d in enumerate(order):
        table[d] = [order[(i - step) % size] for step in range(size)]
    where = jnp.asarray(table, jnp.int32)[lax.axis_index("fsdp")]
    tile = hidden
    halves = 2

    flat_rows = tokens.reshape(examples * seq_len, width)
    flat_grads = hidden_grad.reshape(examples * seq_len, hidden)
    own = open_pack(lengths, flat_rows, examples, seq_len, halves)
    proj_t, out_t = in_proj.T, out_proj.T

    right, left = list(own), list(own)
    state = None
    for step in range(1, half):
        for h in range(halves):
            o = 1 - h
            if step == 2 and h == 0:
                right[h], left[o], state, grads, other = lax.optimization_barrier((right[h], left[o], state, grads, other))
            elif step > 1:
                right[h], left[o], state = lax.optimization_barrier((right[h], left[o], state))
            xs = [right[h], left[o]]
            right[h] = lax.ppermute(right[h], "fsdp", right_way)
            left[o] = lax.ppermute(left[o], "fsdp", left_way)
            if step > 1:
                parts = [(step - 1, h), (size - step + 1, o)]
                state = absorb(where, parts, xs, gate_weight, proj_t, state, tile)
        if step == 1:
            state = absorb(where, [(0, 0), (0, 1)], own, gate_weight, proj_t, None, tile)
            grads = pack(lengths, flat_grads, examples, seq_len, 0, hidden, tile)
            other = lax.ppermute(query_sketch, "dp", [(0, 1), (1, 0)])
    right[0], left[1], state = lax.optimization_barrier((right[0], left[1], state))
    cuts = [(0, CUT), (CUT, LIVE)]
    last = [
        [lax.ppermute(right[0][a:b], "fsdp", right_way), lax.ppermute(left[1][a:b], "fsdp", left_way)]
        for a, b in cuts
    ]
    for h in range(halves):
        parts = [(half - 1, h), (size - half + 1, 1 - h)]
        final = half if h == halves - 1 else None
        state = absorb(where, parts, [right[h], left[1 - h]], gate_weight, proj_t, state, tile, final)
    *state, last_weight = state
    total = None
    for xs, (a, _) in zip(last, cuts, strict=True):
        total = finish(
            where, lengths, xs, last_weight, proj_t, state, grads, out_t, total, half, a, examples, seq_len
        )
    for hops in reduce_hops(size):
        held = total
        for hop in hops:
            total = total + lax.ppermute(held, "fsdp", [(i, i ^ hop) for i in range(size)])
    sketch = total.reshape(rank_in, examples, rank_out).transpose(1, 0, 2)
    sketch = sketch.reshape(examples, rank_in * rank_out)
    share = sketch.shape[1] // size
    own_cols = lax.dynamic_slice_in_dim(sketch, lax.axis_index("fsdp") * share, share, 1)
    first = lax.axis_index("dp") == 0
    queries = jnp.concatenate(
        [jnp.where(first, query_sketch, other), jnp.where(first, other, query_sketch)], axis=1
    )
    scores = jnp.einsum(
        "ek,qk->eq", sketch.astype(jnp.bfloat16), queries, preferred_element_type=jnp.float32
    )
    return (own_cols, scores)


def solution(mesh):
    order = ring_order(mesh.shape["fsdp"], folded=mesh.shape["parts"] == 2)

    def per_device(*args):
        return on_device(order, *args)

    return jax.shard_map(
        per_device,
        mesh=mesh,
        in_specs=(
            P(("parts", "dp"), None, "fsdp"),
            P(("parts", "dp"), None),
            P(None, "fsdp"),
            P(("parts", "dp"), None, "fsdp"),
            P(),
            P("fsdp", None),
            P("fsdp", "dp"),
        ),
        out_specs=(P(("parts", "dp"), "fsdp"), P(("parts", "dp"), "fsdp")),
        check_vma=False,
    )
```

```python
import functools
import math

import jax
import jax.numpy as jnp
from jax import lax
from jax.experimental import pallas as pl
from jax.experimental.pallas import tpu as pltpu
from jax.sharding import PartitionSpec as P

LIVE = 640
CUT = 384
WHOLE = 60 << 20
SMALL = 12 << 20
LARGE = 38 << 20
NT = (((1,), (1,)), ((), ()))
TN = (((0,), (0,)), ((), ()))


def ring_order(size, folded):
    if folded:
        return list(range(0, size, 2)) + list(range(size - 1, 0, -2))
    return list(range(size))


def reduce_hops(size):
    rounds, hop = [], 1
    while hop < size:
        rounds.append((hop, 2 * hop, 3 * hop) if 2 * hop < size else (hop,))
        hop *= 4
    return rounds


def dot(a, b):
    return jnp.dot(a, b, preferred_element_type=jnp.float32)


def row_sources(lens, examples, seq_len):
    row = lax.broadcasted_iota(jnp.int32, (LIVE, 1), 0)
    slot, owner, start = row, jnp.zeros_like(row), jnp.int32(0)
    for e in range(1, examples):
        start = start + lens[0, e - 1]
        slot = jnp.where(row >= start, row - start + e * seq_len, slot)
        owner = jnp.where(row >= start, e, owner)
    return slot, owner


def pack_kernel(examples, seq_len, lens, x_ref, out_ref, pick):
    @pl.when(pl.program_id(0) == 0)
    def _():
        slot, _ = row_sources(lens, examples, seq_len)
        columns = lax.broadcasted_iota(jnp.int32, (LIVE, examples * seq_len), 1)
        pick[...] = jnp.where(columns == slot, 1.0, 0.0).astype(pick.dtype)

    out_ref[...] = dot(pick[...], x_ref[...]).astype(out_ref.dtype)


def pack(lengths, rows, examples, seq_len, first, count, tile):
    slots = rows.shape[0]
    return pl.pallas_call(
        functools.partial(pack_kernel, examples, seq_len),
        out_shape=jax.ShapeDtypeStruct((LIVE, count), rows.dtype),
        grid=(count // tile,),
        in_specs=[
            pl.BlockSpec(memory_space=pltpu.SMEM),
            pl.BlockSpec((slots, tile), lambda j: (0, first // tile + j)),
        ],
        out_specs=pl.BlockSpec((LIVE, tile), lambda j: (0, j)),
        scratch_shapes=[pltpu.VMEM((LIVE, slots), rows.dtype)],
        compiler_params=pltpu.CompilerParams(vmem_limit_bytes=LARGE),
        cost_estimate=pl.CostEstimate(
            flops=2 * LIVE * slots * count, bytes_accessed=2 * (slots + LIVE) * count, transcendentals=0
        ),
    )(lengths, rows)


def project(x, proj_t):
    return lax.dot_general(x, proj_t, NT, preferred_element_type=jnp.float32)


def open_kernel(examples, seq_len, reach, lens_in, x_in, *refs):
    outs, (lens, x, pick, sem) = refs[:-4], refs[-4:]
    count = len(outs)
    slots, width = x.shape
    depth, rows = width // count, LIVE // 2
    lens_copy = pltpu.make_async_copy(lens_in, lens, sem.at[count])
    lens_copy.start()
    loads = []
    for h in range(count):
        columns = slice(h * depth, (h + 1) * depth)
        loads.append(pltpu.make_async_copy(x_in.at[:, columns], x.at[:, columns], sem.at[h]))
        loads[h].start()
    lens_copy.wait()
    slot, _ = row_sources(lens, examples, seq_len)
    for m in range(2):
        columns = lax.broadcasted_iota(jnp.int32, (rows, reach), 1) + m * (slots - reach)
        pick[m] = jnp.where(columns == slot[m * rows : (m + 1) * rows], 1.0, 0.0).astype(pick.dtype)
    for h, out in enumerate(outs):
        loads[h].wait()
        for m in range(2):
            first = m * (slots - reach)
            part = dot(pick[m], x[first : first + reach, h * depth : (h + 1) * depth])
            out[m * rows : (m + 1) * rows, :] = part.astype(out.dtype)


def open_pack(lengths, rows, examples, seq_len, halves):
    slots, width = rows.shape
    reach = -(-(slots - LIVE // 2) // 128) * 128
    return pl.pallas_call(
        functools.partial(open_kernel, examples, seq_len, reach),
        out_shape=[jax.ShapeDtypeStruct((LIVE, width // halves), rows.dtype)] * halves,
        in_specs=[pl.BlockSpec(memory_space=pl.ANY)] * 2,
        out_specs=[pl.BlockSpec(memory_space=pltpu.VMEM)] * halves,
        scratch_shapes=[
            pltpu.SMEM(lengths.shape, lengths.dtype),
            pltpu.VMEM(rows.shape, rows.dtype),
            pltpu.VMEM((2, LIVE // 2, reach), rows.dtype),
            pltpu.SemaphoreType.DMA((halves + 1,)),
        ],
        compiler_params=pltpu.CompilerParams(vmem_limit_bytes=WHOLE),
        cost_estimate=pl.CostEstimate(
            flops=2 * LIVE * slots * width, bytes_accessed=2 * (slots + LIVE) * width, transcendentals=0
        ),
    )(lengths, rows)


def absorb_kernel(parts, first, final, tile, where, *refs):
    count = len(parts)
    xs, (weight, proj_t), refs = refs[:count], refs[count : count + 2], refs[count + 2 :]
    if not first:
        (gate_in, left_in), refs = refs[:2], refs[2:]
    gate, left, *handed, held, sems = refs
    depth = xs[0].shape[1]

    def start_of(step, h):
        return pl.multiple_of(where[step] * (2 * depth) + h * depth, depth)

    copies = []
    for i, (step, h) in enumerate(parts):
        copies.append(pltpu.make_async_copy(weight.at[pl.ds(start_of(step, h), depth), :], held.at[i], sems.at[i]))
    if handed:
        rows = pl.ds(start_of(final, 0), 2 * depth)
        copies.append(pltpu.make_async_copy(weight.at[rows, :], handed[0], sems.at[count]))
    for copy in copies:
        copy.start()
    total = None if first else left_in[...]
    for x, (step, h) in zip(xs, parts, strict=True):
        term = project(x[...], proj_t[:, pl.ds(start_of(step, h), depth)])
        total = term if total is None else total + term
    left[...] = total
    for copy in copies[:count]:
        copy.wait()

    def one(j, carry):
        columns = pl.ds(pl.multiple_of(j * tile, tile), tile)
        total = None if first else gate_in[:, columns]
        for i, x in enumerate(xs):
            term = dot(x[...], held[i, :, columns])
            total = term if total is None else total + term
        gate[:, columns] = total
        return carry

    lax.fori_loop(0, held.shape[2] // tile, one, 0)
    for copy in copies[count:]:
        copy.wait()


def in_vmem(count):
    return [pl.BlockSpec(memory_space=pltpu.VMEM)] * count


def absorb(where, parts, xs, weight, proj_t, state, tile, final=None):
    hidden, rank = weight.shape[1], proj_t.shape[0]
    args = [where, *xs, weight, proj_t, *(state or ())]
    aliases = {} if state is None else {len(args) - 2: 0, len(args) - 1: 1}
    depth, count = xs[0].shape[1], len(xs)
    handed = [] if final is None else [jax.ShapeDtypeStruct((2 * depth, hidden), weight.dtype)]
    return pl.pallas_call(
        functools.partial(absorb_kernel, parts, state is None, final, tile),
        out_shape=[
            jax.ShapeDtypeStruct((LIVE, hidden), jnp.float32),
            jax.ShapeDtypeStruct((LIVE, rank), jnp.float32),
        ]
        + handed,
        in_specs=[pl.BlockSpec(memory_space=pltpu.SMEM)]
        + in_vmem(count)
        + [pl.BlockSpec(memory_space=pltpu.HBM)]
        + in_vmem(len(args) - 2 - count),
        out_specs=in_vmem(2 + len(handed)),
        input_output_aliases=aliases,
        scratch_shapes=[
            pltpu.VMEM((count, depth, hidden), weight.dtype),
            pltpu.SemaphoreType.DMA((count + 1,)),
        ],
        compiler_params=pltpu.CompilerParams(vmem_limit_bytes=LARGE),
        cost_estimate=pl.CostEstimate(
            flops=2 * LIVE * depth * count * (hidden + 256),
            bytes_accessed=2 * depth * count * (hidden + LIVE) + 8 * LIVE * hidden,
            transcendentals=0,
        ),
    )(*args)


def finish_kernel(examples, seq_len, step, first, where, lens, *refs):
    xs, refs = refs[:2], refs[2:]
    weight, proj_t, gate_in, left_in, grads, out_t, *before, sketch, block = refs
    count, depth = xs[0].shape
    rows = slice(first, first + count)
    row = pl.multiple_of(where[step] * (2 * depth), 2 * depth)
    block[:, :depth] = xs[0][...]
    block[:, depth:] = xs[1][...]
    gate = gate_in[rows, :] + dot(block[...], weight[...])
    up_grad = (grads[rows, :].astype(jnp.float32) * jax.nn.silu(gate)).astype(jnp.bfloat16)
    right = project(up_grad, out_t[...])
    left = left_in[rows, :] + project(block[...], proj_t[:, pl.ds(row, 2 * depth)])
    _, owner = row_sources(lens, examples, seq_len)
    owner = owner[rows, :]
    weighted = jnp.concatenate([jnp.where(owner == e, right, 0.0) for e in range(examples)], axis=1)
    term = lax.dot_general(
        left * (1.0 / math.sqrt(seq_len)),
        weighted,
        TN,
        precision=lax.Precision.HIGHEST,
        preferred_element_type=jnp.float32,
    )
    sketch[...] = before[0][...] + term if before else term


def finish(where, lengths, xs, weight, proj_t, state, grads, out_t, before, step, first, examples, seq_len):
    hidden, rank_in, rank_out = weight.shape[1], proj_t.shape[0], out_t.shape[0]
    count, depth = xs[0].shape[0], xs[0].shape[1] * 2
    args = [*xs, weight, proj_t, *state, grads, out_t, *([] if before is None else [before])]
    return pl.pallas_call(
        functools.partial(finish_kernel, examples, seq_len, step, first),
        out_shape=jax.ShapeDtypeStruct((rank_in, examples * rank_out), jnp.float32),
        in_specs=[pl.BlockSpec(memory_space=pltpu.SMEM)] * 2 + in_vmem(len(args)),
        out_specs=pl.BlockSpec(memory_space=pltpu.VMEM),
        scratch_shapes=[pltpu.VMEM((count, depth), jnp.bfloat16)],
        compiler_params=pltpu.CompilerParams(vmem_limit_bytes=SMALL),
        cost_estimate=pl.CostEstimate(
            flops=2 * count * (depth + 256) * (hidden + 256),
            bytes_accessed=2 * depth * (hidden + count) + 6 * count * hidden,
            transcendentals=count * hidden,
        ),
    )(where, lengths, *args)


def score_kernel(share, sketch, queries_t, own_cols, scores):
    place = lax.axis_index("fsdp")
    own_cols[...] = sketch[:, pl.ds(pl.multiple_of(place * share, share), share)]
    scores[...] = dot(sketch[...].astype(jnp.bfloat16), queries_t[...])


def score(sketch, queries_t, size):
    examples, entries = sketch.shape
    share, count = entries // size, queries_t.shape[1]
    return pl.pallas_call(
        functools.partial(score_kernel, share),
        out_shape=[
            jax.ShapeDtypeStruct((examples, share), jnp.float32),
            jax.ShapeDtypeStruct((examples, count), jnp.float32),
        ],
        in_specs=in_vmem(2),
        out_specs=in_vmem(2),
        compiler_params=pltpu.CompilerParams(vmem_limit_bytes=SMALL),
        cost_estimate=pl.CostEstimate(
            flops=2 * examples * entries * count, bytes_accessed=2 * entries * count, transcendentals=0
        ),
    )(sketch, queries_t)


def on_device(order, tokens, lengths, gate_weight, hidden_grad, in_proj, out_proj, query_sketch):
    examples, seq_len, width = tokens.shape
    hidden = hidden_grad.shape[2]
    rank_in, rank_out = in_proj.shape[1], out_proj.shape[1]
    size = len(order)
    half = size // 2
    right_way = [(order[i], order[(i + 1) % size]) for i in range(size)]
    left_way = [(d, s) for s, d in right_way]
    table = [[0] * size for _ in range(size)]
    for i, d in enumerate(order):
        table[d] = [order[(i - step) % size] for step in range(size)]
    where = jnp.asarray(table, jnp.int32)[lax.axis_index("fsdp")]
    tile = hidden
    halves = 2

    flat_rows = tokens.reshape(examples * seq_len, width)
    flat_grads = hidden_grad.reshape(examples * seq_len, hidden)
    own = open_pack(lengths, flat_rows, examples, seq_len, halves)
    proj_t, out_t = in_proj.T, out_proj.T

    right, left = list(own), list(own)
    state = None
    for step in range(1, half):
        for h in range(halves):
            o = 1 - h
            if step == 2 and h == 0:
                right[h], left[o], state, grads = lax.optimization_barrier((right[h], left[o], state, grads))
            elif step == 3 and h == 0:
                right[h], left[o], state, query_sketch = lax.optimization_barrier(
                    (right[h], left[o], state, query_sketch)
                )
            elif step > 1:
                right[h], left[o], state = lax.optimization_barrier((right[h], left[o], state))
            xs = [right[h], left[o]]
            right[h] = lax.ppermute(right[h], "fsdp", right_way)
            left[o] = lax.ppermute(left[o], "fsdp", left_way)
            if step > 1:
                parts = [(step - 1, h), (size - step + 1, o)]
                state = absorb(where, parts, xs, gate_weight, proj_t, state, tile)
        if step == 1:
            state = absorb(where, [(0, 0), (0, 1)], own, gate_weight, proj_t, None, tile)
            grads = pack(lengths, flat_grads, examples, seq_len, 0, hidden, tile)
        if step == 3:
            other = lax.ppermute(query_sketch, "dp", [(0, 1), (1, 0)])
            mine_t, other_t = query_sketch.T, other.T
            first = lax.axis_index("dp") == 0
            queries_t = jnp.concatenate(
                [jnp.where(first, mine_t, other_t), jnp.where(first, other_t, mine_t)], axis=0
            )
    right[0], left[1], state, queries_t = lax.optimization_barrier((right[0], left[1], state, queries_t))
    cuts = [(0, CUT), (CUT, LIVE)]
    ends = [right[0], left[1]]
    last = [[lax.ppermute(ends[0][:CUT], "fsdp", right_way), lax.ppermute(ends[1][:CUT], "fsdp", left_way)]]
    for h in range(halves):
        parts = [(half - 1, h), (size - half + 1, 1 - h)]
        final = half if h == halves - 1 else None
        state = absorb(where, parts, [right[h], left[1 - h]], gate_weight, proj_t, state, tile, final)
        if h == 0:
            *ends, state = lax.optimization_barrier((ends[0][CUT:], ends[1][CUT:], state))
            last.append([lax.ppermute(ends[0], "fsdp", right_way), lax.ppermute(ends[1], "fsdp", left_way)])
    *state, last_weight = state
    total = None
    for xs, (a, _) in zip(last, cuts, strict=True):
        total = finish(
            where, lengths, xs, last_weight, proj_t, state, grads, out_t, total, half, a, examples, seq_len
        )
    for hops in reduce_hops(size):
        low = total.astype(jnp.bfloat16)
        for hop in hops:
            total = total + lax.ppermute(low, "fsdp", [(i, i ^ hop) for i in range(size)]).astype(jnp.float32)
    sketch = total.reshape(rank_in, examples, rank_out).transpose(1, 0, 2)
    sketch = sketch.reshape(examples, rank_in * rank_out)
    return score(sketch, queries_t, size)


def solution(mesh):
    order = ring_order(mesh.shape["fsdp"], folded=mesh.shape["parts"] == 2)

    def per_device(*args):
        return on_device(order, *args)

    return jax.shard_map(
        per_device,
        mesh=mesh,
        in_specs=(
            P(("parts", "dp"), None, "fsdp"),
            P(("parts", "dp"), None),
            P(None, "fsdp"),
            P(("parts", "dp"), None, "fsdp"),
            P(),
            P("fsdp", None),
            P("fsdp", "dp"),
        ),
        out_specs=(P(("parts", "dp"), "fsdp"), P(("parts", "dp"), "fsdp")),
        check_vma=False,
    )
```

```python
import functools
import math

import jax
import jax.numpy as jnp
from jax import lax
from jax.experimental import pallas as pl
from jax.experimental.pallas import tpu as pltpu
from jax.sharding import PartitionSpec as P

LIVE = 640
CUT = 384
WHOLE = 60 << 20
SMALL = 12 << 20
LARGE = 38 << 20
NT = (((1,), (1,)), ((), ()))
TN = (((0,), (0,)), ((), ()))


def ring_order(size, folded):
    if folded:
        return list(range(0, size, 2)) + list(range(size - 1, 0, -2))
    return list(range(size))


def reduce_hops(size):
    rounds, hop = [], 1
    while hop < size:
        rounds.append((hop, 2 * hop, 3 * hop) if 2 * hop < size else (hop,))
        hop *= 4
    return rounds


def dot(a, b):
    return jnp.dot(a, b, preferred_element_type=jnp.float32)


def row_sources(lens, examples, seq_len):
    row = lax.broadcasted_iota(jnp.int32, (LIVE, 1), 0)
    slot, owner, start = row, jnp.zeros_like(row), jnp.int32(0)
    for e in range(1, examples):
        start = start + lens[0, e - 1]
        slot = jnp.where(row >= start, row - start + e * seq_len, slot)
        owner = jnp.where(row >= start, e, owner)
    return slot, owner


def pack_kernel(examples, seq_len, lens, x_ref, out_ref, pick):
    @pl.when(pl.program_id(0) == 0)
    def _():
        slot, _ = row_sources(lens, examples, seq_len)
        columns = lax.broadcasted_iota(jnp.int32, (LIVE, examples * seq_len), 1)
        pick[...] = jnp.where(columns == slot, 1.0, 0.0).astype(pick.dtype)

    out_ref[...] = dot(pick[...], x_ref[...]).astype(out_ref.dtype)


def pack(lengths, rows, examples, seq_len, first, count, tile):
    slots = rows.shape[0]
    return pl.pallas_call(
        functools.partial(pack_kernel, examples, seq_len),
        out_shape=jax.ShapeDtypeStruct((LIVE, count), rows.dtype),
        grid=(count // tile,),
        in_specs=[
            pl.BlockSpec(memory_space=pltpu.SMEM),
            pl.BlockSpec((slots, tile), lambda j: (0, first // tile + j)),
        ],
        out_specs=pl.BlockSpec((LIVE, tile), lambda j: (0, j)),
        scratch_shapes=[pltpu.VMEM((LIVE, slots), rows.dtype)],
        compiler_params=pltpu.CompilerParams(vmem_limit_bytes=LARGE),
        cost_estimate=pl.CostEstimate(
            flops=2 * LIVE * slots * count, bytes_accessed=2 * (slots + LIVE) * count, transcendentals=0
        ),
    )(lengths, rows)


def project(x, proj_t):
    return lax.dot_general(x, proj_t, NT, preferred_element_type=jnp.float32)


def open_kernel(examples, seq_len, reach, lens_in, x_in, *refs):
    outs, (lens, x, pick, sem) = refs[:-4], refs[-4:]
    count = len(outs)
    slots, width = x.shape
    depth, rows = width // count, LIVE // 2
    lens_copy = pltpu.make_async_copy(lens_in, lens, sem.at[count])
    lens_copy.start()
    loads = []
    for h in range(count):
        columns = slice(h * depth, (h + 1) * depth)
        loads.append(pltpu.make_async_copy(x_in.at[:, columns], x.at[:, columns], sem.at[h]))
        loads[h].start()
    lens_copy.wait()
    slot, _ = row_sources(lens, examples, seq_len)
    for m in range(2):
        columns = lax.broadcasted_iota(jnp.int32, (rows, reach), 1) + m * (slots - reach)
        pick[m] = jnp.where(columns == slot[m * rows : (m + 1) * rows], 1.0, 0.0).astype(pick.dtype)
    for h, out in enumerate(outs):
        loads[h].wait()
        for m in range(2):
            first = m * (slots - reach)
            part = dot(pick[m], x[first : first + reach, h * depth : (h + 1) * depth])
            out[m * rows : (m + 1) * rows, :] = part.astype(out.dtype)


def open_pack(lengths, rows, examples, seq_len, halves):
    slots, width = rows.shape
    reach = -(-(slots - LIVE // 2) // 128) * 128
    return pl.pallas_call(
        functools.partial(open_kernel, examples, seq_len, reach),
        out_shape=[jax.ShapeDtypeStruct((LIVE, width // halves), rows.dtype)] * halves,
        in_specs=[pl.BlockSpec(memory_space=pl.ANY)] * 2,
        out_specs=[pl.BlockSpec(memory_space=pltpu.VMEM)] * halves,
        scratch_shapes=[
            pltpu.SMEM(lengths.shape, lengths.dtype),
            pltpu.VMEM(rows.shape, rows.dtype),
            pltpu.VMEM((2, LIVE // 2, reach), rows.dtype),
            pltpu.SemaphoreType.DMA((halves + 1,)),
        ],
        compiler_params=pltpu.CompilerParams(vmem_limit_bytes=WHOLE),
        cost_estimate=pl.CostEstimate(
            flops=2 * LIVE * slots * width, bytes_accessed=2 * (slots + LIVE) * width, transcendentals=0
        ),
    )(lengths, rows)


def absorb_kernel(parts, first, final, tile, where, *refs):
    count = len(parts)
    xs, (weight, proj_t), refs = refs[:count], refs[count : count + 2], refs[count + 2 :]
    if not first:
        (gate_in, left_in), refs = refs[:2], refs[2:]
    gate, left, *handed, held, sems = refs
    depth = xs[0].shape[1]

    def start_of(step, h):
        return pl.multiple_of(where[step] * (2 * depth) + h * depth, depth)

    copies = []
    for i, (step, h) in enumerate(parts):
        copies.append(pltpu.make_async_copy(weight.at[pl.ds(start_of(step, h), depth), :], held.at[i], sems.at[i]))
    if handed:
        rows = pl.ds(start_of(final, 0), 2 * depth)
        copies.append(pltpu.make_async_copy(weight.at[rows, :], handed[0], sems.at[count]))
    for copy in copies:
        copy.start()
    total = None if first else left_in[...]
    for x, (step, h) in zip(xs, parts, strict=True):
        term = project(x[...], proj_t[:, pl.ds(start_of(step, h), depth)])
        total = term if total is None else total + term
    left[...] = total
    for copy in copies[:count]:
        copy.wait()

    def one(j, carry):
        columns = pl.ds(pl.multiple_of(j * tile, tile), tile)
        total = None if first else gate_in[:, columns]
        for i, x in enumerate(xs):
            term = dot(x[...], held[i, :, columns])
            total = term if total is None else total + term
        gate[:, columns] = total
        return carry

    lax.fori_loop(0, held.shape[2] // tile, one, 0)
    for copy in copies[count:]:
        copy.wait()


def in_vmem(count):
    return [pl.BlockSpec(memory_space=pltpu.VMEM)] * count


def absorb(where, parts, xs, weight, proj_t, state, tile, final=None):
    hidden, rank = weight.shape[1], proj_t.shape[0]
    args = [where, *xs, weight, proj_t, *(state or ())]
    aliases = {} if state is None else {len(args) - 2: 0, len(args) - 1: 1}
    depth, count = xs[0].shape[1], len(xs)
    handed = [] if final is None else [jax.ShapeDtypeStruct((2 * depth, hidden), weight.dtype)]
    return pl.pallas_call(
        functools.partial(absorb_kernel, parts, state is None, final, tile),
        out_shape=[
            jax.ShapeDtypeStruct((LIVE, hidden), jnp.float32),
            jax.ShapeDtypeStruct((LIVE, rank), jnp.float32),
        ]
        + handed,
        in_specs=[pl.BlockSpec(memory_space=pltpu.SMEM)]
        + in_vmem(count)
        + [pl.BlockSpec(memory_space=pltpu.HBM)]
        + in_vmem(len(args) - 2 - count),
        out_specs=in_vmem(2 + len(handed)),
        input_output_aliases=aliases,
        scratch_shapes=[
            pltpu.VMEM((count, depth, hidden), weight.dtype),
            pltpu.SemaphoreType.DMA((count + 1,)),
        ],
        compiler_params=pltpu.CompilerParams(vmem_limit_bytes=LARGE),
        cost_estimate=pl.CostEstimate(
            flops=2 * LIVE * depth * count * (hidden + 256),
            bytes_accessed=2 * depth * count * (hidden + LIVE) + 8 * LIVE * hidden,
            transcendentals=0,
        ),
    )(*args)


def finish_kernel(examples, seq_len, step, first, where, lens, *refs):
    xs, refs = refs[:2], refs[2:]
    weight, proj_t, gate_in, left_in, grads, out_t, *before, sketch, block = refs
    count, depth = xs[0].shape
    rows = slice(first, first + count)
    row = pl.multiple_of(where[step] * (2 * depth), 2 * depth)
    block[:, :depth] = xs[0][...]
    block[:, depth:] = xs[1][...]
    gate = gate_in[rows, :] + dot(block[...], weight[...])
    up_grad = (grads[rows, :].astype(jnp.float32) * jax.nn.silu(gate)).astype(jnp.bfloat16)
    right = project(up_grad, out_t[...])
    left = left_in[rows, :] + project(block[...], proj_t[:, pl.ds(row, 2 * depth)])
    _, owner = row_sources(lens, examples, seq_len)
    owner = owner[rows, :]
    weighted = jnp.concatenate([jnp.where(owner == e, right, 0.0) for e in range(examples)], axis=1)
    term = lax.dot_general(
        left * (1.0 / math.sqrt(seq_len)),
        weighted,
        TN,
        precision=lax.Precision.HIGHEST,
        preferred_element_type=jnp.float32,
    )
    sketch[...] = before[0][...] + term if before else term


def finish(where, lengths, xs, weight, proj_t, state, grads, out_t, before, step, first, examples, seq_len):
    hidden, rank_in, rank_out = weight.shape[1], proj_t.shape[0], out_t.shape[0]
    count, depth = xs[0].shape[0], xs[0].shape[1] * 2
    args = [*xs, weight, proj_t, *state, grads, out_t, *([] if before is None else [before])]
    return pl.pallas_call(
        functools.partial(finish_kernel, examples, seq_len, step, first),
        out_shape=jax.ShapeDtypeStruct((rank_in, examples * rank_out), jnp.float32),
        in_specs=[pl.BlockSpec(memory_space=pltpu.SMEM)] * 2 + in_vmem(len(args)),
        out_specs=pl.BlockSpec(memory_space=pltpu.VMEM),
        scratch_shapes=[pltpu.VMEM((count, depth), jnp.bfloat16)],
        compiler_params=pltpu.CompilerParams(vmem_limit_bytes=SMALL),
        cost_estimate=pl.CostEstimate(
            flops=2 * count * (depth + 256) * (hidden + 256),
            bytes_accessed=2 * depth * (hidden + count) + 6 * count * hidden,
            transcendentals=count * hidden,
        ),
    )(where, lengths, *args)


def score_kernel(share, sketch, queries_t, own_cols, scores):
    place = lax.axis_index("fsdp")
    own_cols[...] = sketch[:, pl.ds(pl.multiple_of(place * share, share), share)]
    scores[...] = dot(sketch[...].astype(jnp.bfloat16), queries_t[...])


def score(sketch, queries_t, size):
    examples, entries = sketch.shape
    share, count = entries // size, queries_t.shape[1]
    return pl.pallas_call(
        functools.partial(score_kernel, share),
        out_shape=[
            jax.ShapeDtypeStruct((examples, share), jnp.float32),
            jax.ShapeDtypeStruct((examples, count), jnp.float32),
        ],
        in_specs=in_vmem(2),
        out_specs=in_vmem(2),
        compiler_params=pltpu.CompilerParams(vmem_limit_bytes=SMALL),
        cost_estimate=pl.CostEstimate(
            flops=2 * examples * entries * count, bytes_accessed=2 * entries * count, transcendentals=0
        ),
    )(sketch, queries_t)


def on_device(order, tokens, lengths, gate_weight, hidden_grad, in_proj, out_proj, query_sketch):
    examples, seq_len, width = tokens.shape
    hidden = hidden_grad.shape[2]
    rank_in, rank_out = in_proj.shape[1], out_proj.shape[1]
    size = len(order)
    half = size // 2
    right_way = [(order[i], order[(i + 1) % size]) for i in range(size)]
    left_way = [(d, s) for s, d in right_way]
    table = [[0] * size for _ in range(size)]
    for i, d in enumerate(order):
        table[d] = [order[(i - step) % size] for step in range(size)]
    where = jnp.asarray(table, jnp.int32)[lax.axis_index("fsdp")]
    tile = hidden
    halves = 2

    flat_rows = tokens.reshape(examples * seq_len, width)
    flat_grads = hidden_grad.reshape(examples * seq_len, hidden)
    own = open_pack(lengths, flat_rows, examples, seq_len, halves)
    proj_t, out_t = in_proj.T, out_proj.T

    right, left = list(own), list(own)
    state = None
    for step in range(1, half):
        for h in range(halves):
            o = 1 - h
            if step == 2 and h == 0:
                right[h], left[o], state, grads = lax.optimization_barrier((right[h], left[o], state, grads))
            elif step == 3 and h == 0:
                right[h], left[o], state, query_sketch = lax.optimization_barrier(
                    (right[h], left[o], state, query_sketch)
                )
            elif step > 1:
                right[h], left[o], state = lax.optimization_barrier((right[h], left[o], state))
            xs = [right[h], left[o]]
            right[h] = lax.ppermute(right[h], "fsdp", right_way)
            left[o] = lax.ppermute(left[o], "fsdp", left_way)
            if step > 1:
                parts = [(step - 1, h), (size - step + 1, o)]
                state = absorb(where, parts, xs, gate_weight, proj_t, state, tile)
        if step == 1:
            state = absorb(where, [(0, 0), (0, 1)], own, gate_weight, proj_t, None, tile)
            grads = pack(lengths, flat_grads, examples, seq_len, 0, hidden, tile)
        if step == 3:
            other = lax.ppermute(query_sketch, "dp", [(0, 1), (1, 0)])
            mine_t, other_t = query_sketch.T, other.T
            first = lax.axis_index("dp") == 0
            queries_t = jnp.concatenate(
                [jnp.where(first, mine_t, other_t), jnp.where(first, other_t, mine_t)], axis=0
            )
    right[0], left[1], state, queries_t = lax.optimization_barrier((right[0], left[1], state, queries_t))
    cuts = [(0, CUT), (CUT, LIVE)]
    ends = [right[0], left[1]]
    last = [[lax.ppermute(ends[0][:CUT], "fsdp", right_way), lax.ppermute(ends[1][:CUT], "fsdp", left_way)]]
    for h in range(halves):
        parts = [(half - 1, h), (size - half + 1, 1 - h)]
        final = half if h == halves - 1 else None
        state = absorb(where, parts, [right[h], left[1 - h]], gate_weight, proj_t, state, tile, final)
        if h == 0:
            *ends, state = lax.optimization_barrier((ends[0][CUT:], ends[1][CUT:], state))
            last.append([lax.ppermute(ends[0], "fsdp", right_way), lax.ppermute(ends[1], "fsdp", left_way)])
    *state, last_weight = state
    total = None
    for xs, (a, _) in zip(last, cuts, strict=True):
        total = finish(
            where, lengths, xs, last_weight, proj_t, state, grads, out_t, total, half, a, examples, seq_len
        )
    for hops in reduce_hops(size):
        held = total
        for hop in hops:
            total = total + lax.ppermute(held, "fsdp", [(i, i ^ hop) for i in range(size)])
    sketch = total.reshape(rank_in, examples, rank_out).transpose(1, 0, 2)
    sketch = sketch.reshape(examples, rank_in * rank_out)
    return score(sketch, queries_t, size)


def solution(mesh):
    order = ring_order(mesh.shape["fsdp"], folded=mesh.shape["parts"] == 2)

    def per_device(*args):
        return on_device(order, *args)

    return jax.shard_map(
        per_device,
        mesh=mesh,
        in_specs=(
            P(("parts", "dp"), None, "fsdp"),
            P(("parts", "dp"), None),
            P(None, "fsdp"),
            P(("parts", "dp"), None, "fsdp"),
            P(),
            P("fsdp", None),
            P("fsdp", "dp"),
        ),
        out_specs=(P(("parts", "dp"), "fsdp"), P(("parts", "dp"), "fsdp")),
        check_vma=False,
    )
```

```python
import functools
import math

import jax
import jax.numpy as jnp
from jax import lax
from jax.experimental import pallas as pl
from jax.experimental.pallas import tpu as pltpu
from jax.sharding import PartitionSpec as P

LIVE = 640
CUT = 416
WHOLE = 60 << 20
SMALL = 12 << 20
LARGE = 38 << 20
NT = (((1,), (1,)), ((), ()))
TN = (((0,), (0,)), ((), ()))


def ring_order(size, folded):
    if folded:
        return list(range(0, size, 2)) + list(range(size - 1, 0, -2))
    return list(range(size))


def reduce_hops(size):
    rounds, hop = [], 1
    while hop < size:
        rounds.append((hop, 2 * hop, 3 * hop) if 2 * hop < size else (hop,))
        hop *= 4
    return rounds


def dot(a, b):
    return jnp.dot(a, b, preferred_element_type=jnp.float32)


def row_sources(lens, examples, seq_len):
    row = lax.broadcasted_iota(jnp.int32, (LIVE, 1), 0)
    slot, owner, start = row, jnp.zeros_like(row), jnp.int32(0)
    for e in range(1, examples):
        start = start + lens[0, e - 1]
        slot = jnp.where(row >= start, row - start + e * seq_len, slot)
        owner = jnp.where(row >= start, e, owner)
    return slot, owner


def pack_kernel(examples, seq_len, lens, x_ref, out_ref, pick):
    @pl.when(pl.program_id(0) == 0)
    def _():
        slot, _ = row_sources(lens, examples, seq_len)
        columns = lax.broadcasted_iota(jnp.int32, (LIVE, examples * seq_len), 1)
        pick[...] = jnp.where(columns == slot, 1.0, 0.0).astype(pick.dtype)

    out_ref[...] = dot(pick[...], x_ref[...]).astype(out_ref.dtype)


def pack(lengths, rows, examples, seq_len, first, count, tile):
    slots = rows.shape[0]
    return pl.pallas_call(
        functools.partial(pack_kernel, examples, seq_len),
        out_shape=jax.ShapeDtypeStruct((LIVE, count), rows.dtype),
        grid=(count // tile,),
        in_specs=[
            pl.BlockSpec(memory_space=pltpu.SMEM),
            pl.BlockSpec((slots, tile), lambda j: (0, first // tile + j)),
        ],
        out_specs=pl.BlockSpec((LIVE, tile), lambda j: (0, j)),
        scratch_shapes=[pltpu.VMEM((LIVE, slots), rows.dtype)],
        compiler_params=pltpu.CompilerParams(vmem_limit_bytes=LARGE),
        cost_estimate=pl.CostEstimate(
            flops=2 * LIVE * slots * count, bytes_accessed=2 * (slots + LIVE) * count, transcendentals=0
        ),
    )(lengths, rows)


def project(x, proj_t):
    return lax.dot_general(x, proj_t, NT, preferred_element_type=jnp.float32)


def open_kernel(examples, seq_len, reach, lens_in, x_in, *refs):
    outs, (lens, x, pick, sem) = refs[:-4], refs[-4:]
    count = len(outs)
    slots, width = x.shape
    depth, rows = width // count, LIVE // 2
    lens_copy = pltpu.make_async_copy(lens_in, lens, sem.at[count])
    lens_copy.start()
    loads = []
    for h in range(count):
        columns = slice(h * depth, (h + 1) * depth)
        loads.append(pltpu.make_async_copy(x_in.at[:, columns], x.at[:, columns], sem.at[h]))
        loads[h].start()
    lens_copy.wait()
    slot, _ = row_sources(lens, examples, seq_len)
    for m in range(2):
        columns = lax.broadcasted_iota(jnp.int32, (rows, reach), 1) + m * (slots - reach)
        pick[m] = jnp.where(columns == slot[m * rows : (m + 1) * rows], 1.0, 0.0).astype(pick.dtype)
    for h, out in enumerate(outs):
        loads[h].wait()
        for m in range(2):
            first = m * (slots - reach)
            part = dot(pick[m], x[first : first + reach, h * depth : (h + 1) * depth])
            out[m * rows : (m + 1) * rows, :] = part.astype(out.dtype)


def open_pack(lengths, rows, examples, seq_len, halves):
    slots, width = rows.shape
    reach = -(-(slots - LIVE // 2) // 128) * 128
    return pl.pallas_call(
        functools.partial(open_kernel, examples, seq_len, reach),
        out_shape=[jax.ShapeDtypeStruct((LIVE, width // halves), rows.dtype)] * halves,
        in_specs=[pl.BlockSpec(memory_space=pl.ANY)] * 2,
        out_specs=[pl.BlockSpec(memory_space=pltpu.VMEM)] * halves,
        scratch_shapes=[
            pltpu.SMEM(lengths.shape, lengths.dtype),
            pltpu.VMEM(rows.shape, rows.dtype),
            pltpu.VMEM((2, LIVE // 2, reach), rows.dtype),
            pltpu.SemaphoreType.DMA((halves + 1,)),
        ],
        compiler_params=pltpu.CompilerParams(vmem_limit_bytes=WHOLE),
        cost_estimate=pl.CostEstimate(
            flops=2 * LIVE * slots * width, bytes_accessed=2 * (slots + LIVE) * width, transcendentals=0
        ),
    )(lengths, rows)


def absorb_kernel(parts, first, final, tile, where, *refs):
    count = len(parts)
    xs, (weight, proj_t), refs = refs[:count], refs[count : count + 2], refs[count + 2 :]
    if not first:
        (gate_in, left_in), refs = refs[:2], refs[2:]
    gate, left, *handed, held, sems = refs
    depth = xs[0].shape[1]

    def start_of(step, h):
        return pl.multiple_of(where[step] * (2 * depth) + h * depth, depth)

    copies = []
    for i, (step, h) in enumerate(parts):
        copies.append(pltpu.make_async_copy(weight.at[pl.ds(start_of(step, h), depth), :], held.at[i], sems.at[i]))
    if handed:
        rows = pl.ds(start_of(final, 0), 2 * depth)
        copies.append(pltpu.make_async_copy(weight.at[rows, :], handed[0], sems.at[count]))
    for copy in copies:
        copy.start()
    total = None if first else left_in[...]
    for x, (step, h) in zip(xs, parts, strict=True):
        term = project(x[...], proj_t[:, pl.ds(start_of(step, h), depth)])
        total = term if total is None else total + term
    left[...] = total
    for copy in copies[:count]:
        copy.wait()

    def one(j, carry):
        columns = pl.ds(pl.multiple_of(j * tile, tile), tile)
        total = None if first else gate_in[:, columns]
        for i, x in enumerate(xs):
            term = dot(x[...], held[i, :, columns])
            total = term if total is None else total + term
        gate[:, columns] = total
        return carry

    lax.fori_loop(0, held.shape[2] // tile, one, 0)
    for copy in copies[count:]:
        copy.wait()


def in_vmem(count):
    return [pl.BlockSpec(memory_space=pltpu.VMEM)] * count


def absorb(where, parts, xs, weight, proj_t, state, tile, final=None):
    hidden, rank = weight.shape[1], proj_t.shape[0]
    args = [where, *xs, weight, proj_t, *(state or ())]
    aliases = {} if state is None else {len(args) - 2: 0, len(args) - 1: 1}
    depth, count = xs[0].shape[1], len(xs)
    handed = [] if final is None else [jax.ShapeDtypeStruct((2 * depth, hidden), weight.dtype)]
    return pl.pallas_call(
        functools.partial(absorb_kernel, parts, state is None, final, tile),
        out_shape=[
            jax.ShapeDtypeStruct((LIVE, hidden), jnp.float32),
            jax.ShapeDtypeStruct((LIVE, rank), jnp.float32),
        ]
        + handed,
        in_specs=[pl.BlockSpec(memory_space=pltpu.SMEM)]
        + in_vmem(count)
        + [pl.BlockSpec(memory_space=pltpu.HBM)]
        + in_vmem(len(args) - 2 - count),
        out_specs=in_vmem(2 + len(handed)),
        input_output_aliases=aliases,
        scratch_shapes=[
            pltpu.VMEM((count, depth, hidden), weight.dtype),
            pltpu.SemaphoreType.DMA((count + 1,)),
        ],
        compiler_params=pltpu.CompilerParams(vmem_limit_bytes=LARGE),
        cost_estimate=pl.CostEstimate(
            flops=2 * LIVE * depth * count * (hidden + 256),
            bytes_accessed=2 * depth * count * (hidden + LIVE) + 8 * LIVE * hidden,
            transcendentals=0,
        ),
    )(*args)


def two_terms(a):
    high = a.astype(jnp.bfloat16)
    return high, (a - high.astype(jnp.float32)).astype(jnp.bfloat16)


def turned(a, b):
    return lax.dot_general(a, b, TN, preferred_element_type=jnp.float32)


def finish_kernel(examples, seq_len, step, first, where, lens, *refs):
    xs, refs = refs[:2], refs[2:]
    weight, proj_t, gate_in, left_in, grads, out_t, *before, sketch, block = refs
    count, depth = xs[0].shape
    rows = slice(first, first + count)
    row = pl.multiple_of(where[step] * (2 * depth), 2 * depth)
    block[:, :depth] = xs[0][...]
    block[:, depth:] = xs[1][...]
    gate = gate_in[rows, :] + dot(block[...], weight[...])
    up_grad = (grads[rows, :].astype(jnp.float32) * jax.nn.silu(gate)).astype(jnp.bfloat16)
    right = project(up_grad, out_t[...])
    left = left_in[rows, :] + project(block[...], proj_t[:, pl.ds(row, 2 * depth)])
    _, owner = row_sources(lens, examples, seq_len)
    owner = owner[rows, :]
    weighted = jnp.concatenate([jnp.where(owner == e, right, 0.0) for e in range(examples)], axis=1)
    left = left * (1.0 / math.sqrt(seq_len))
    rank = left.shape[1]
    left_high, left_low = two_terms(left)
    high, low = two_terms(weighted)
    both = turned(jnp.concatenate([left_high, left_low], axis=1), high)
    term = both[:rank, :] + both[rank:, :] + turned(left_high, low)
    sketch[...] = before[0][...] + term if before else term


def finish(where, lengths, xs, weight, proj_t, state, grads, out_t, before, step, first, examples, seq_len):
    hidden, rank_in, rank_out = weight.shape[1], proj_t.shape[0], out_t.shape[0]
    count, depth = xs[0].shape[0], xs[0].shape[1] * 2
    args = [*xs, weight, proj_t, *state, grads, out_t, *([] if before is None else [before])]
    return pl.pallas_call(
        functools.partial(finish_kernel, examples, seq_len, step, first),
        out_shape=jax.ShapeDtypeStruct((rank_in, examples * rank_out), jnp.float32),
        in_specs=[pl.BlockSpec(memory_space=pltpu.SMEM)] * 2 + in_vmem(len(args)),
        out_specs=pl.BlockSpec(memory_space=pltpu.VMEM),
        scratch_shapes=[pltpu.VMEM((count, depth), jnp.bfloat16)],
        compiler_params=pltpu.CompilerParams(vmem_limit_bytes=SMALL),
        cost_estimate=pl.CostEstimate(
            flops=2 * count * (depth + 256) * (hidden + 256),
            bytes_accessed=2 * depth * (hidden + count) + 6 * count * hidden,
            transcendentals=count * hidden,
        ),
    )(where, lengths, *args)


def score_kernel(share, sketch, queries_t, own_cols, scores):
    place = lax.axis_index("fsdp")
    own_cols[...] = sketch[:, pl.ds(pl.multiple_of(place * share, share), share)]
    scores[...] = dot(sketch[...].astype(jnp.bfloat16), queries_t[...])


def score(sketch, queries_t, size):
    examples, entries = sketch.shape
    share, count = entries // size, queries_t.shape[1]
    return pl.pallas_call(
        functools.partial(score_kernel, share),
        out_shape=[
            jax.ShapeDtypeStruct((examples, share), jnp.float32),
            jax.ShapeDtypeStruct((examples, count), jnp.float32),
        ],
        in_specs=in_vmem(2),
        out_specs=in_vmem(2),
        compiler_params=pltpu.CompilerParams(vmem_limit_bytes=SMALL),
        cost_estimate=pl.CostEstimate(
            flops=2 * examples * entries * count, bytes_accessed=2 * entries * count, transcendentals=0
        ),
    )(sketch, queries_t)


def on_device(order, tokens, lengths, gate_weight, hidden_grad, in_proj, out_proj, query_sketch):
    examples, seq_len, width = tokens.shape
    hidden = hidden_grad.shape[2]
    rank_in, rank_out = in_proj.shape[1], out_proj.shape[1]
    size = len(order)
    half = size // 2
    right_way = [(order[i], order[(i + 1) % size]) for i in range(size)]
    left_way = [(d, s) for s, d in right_way]
    table = [[0] * size for _ in range(size)]
    for i, d in enumerate(order):
        table[d] = [order[(i - step) % size] for step in range(size)]
    where = jnp.asarray(table, jnp.int32)[lax.axis_index("fsdp")]
    tile = hidden
    halves = 2

    flat_rows = tokens.reshape(examples * seq_len, width)
    flat_grads = hidden_grad.reshape(examples * seq_len, hidden)
    own = open_pack(lengths, flat_rows, examples, seq_len, halves)
    proj_t, out_t = in_proj.T, out_proj.T

    right, left = list(own), list(own)
    state = None
    for step in range(1, half):
        for h in range(halves):
            o = 1 - h
            if step == 2 and h == 0:
                right[h], left[o], state, grads = lax.optimization_barrier((right[h], left[o], state, grads))
            elif step == 3 and h == 0:
                right[h], left[o], state, query_sketch = lax.optimization_barrier(
                    (right[h], left[o], state, query_sketch)
                )
            elif step > 1:
                right[h], left[o], state = lax.optimization_barrier((right[h], left[o], state))
            xs = [right[h], left[o]]
            right[h] = lax.ppermute(right[h], "fsdp", right_way)
            left[o] = lax.ppermute(left[o], "fsdp", left_way)
            if step > 1:
                parts = [(step - 1, h), (size - step + 1, o)]
                state = absorb(where, parts, xs, gate_weight, proj_t, state, tile)
        if step == 1:
            state = absorb(where, [(0, 0), (0, 1)], own, gate_weight, proj_t, None, tile)
            grads = pack(lengths, flat_grads, examples, seq_len, 0, hidden, tile)
        if step == 3:
            other = lax.ppermute(query_sketch, "dp", [(0, 1), (1, 0)])
            mine_t, other_t = query_sketch.T, other.T
            first = lax.axis_index("dp") == 0
            queries_t = jnp.concatenate(
                [jnp.where(first, mine_t, other_t), jnp.where(first, other_t, mine_t)], axis=0
            )
    right[0], left[1], state, queries_t = lax.optimization_barrier((right[0], left[1], state, queries_t))
    cuts = [(0, CUT), (CUT, LIVE)]
    ends = [right[0], left[1]]
    last = [[lax.ppermute(ends[0][:CUT], "fsdp", right_way), lax.ppermute(ends[1][:CUT], "fsdp", left_way)]]
    for h in range(halves):
        parts = [(half - 1, h), (size - half + 1, 1 - h)]
        final = half if h == halves - 1 else None
        state = absorb(where, parts, [right[h], left[1 - h]], gate_weight, proj_t, state, tile, final)
        if h == 0:
            *ends, state = lax.optimization_barrier((ends[0][CUT:], ends[1][CUT:], state))
            last.append([lax.ppermute(ends[0], "fsdp", right_way), lax.ppermute(ends[1], "fsdp", left_way)])
    *state, last_weight = state
    total = None
    for xs, (a, _) in zip(last, cuts, strict=True):
        total = finish(
            where, lengths, xs, last_weight, proj_t, state, grads, out_t, total, half, a, examples, seq_len
        )
    for hops in reduce_hops(size):
        low = total.astype(jnp.bfloat16)
        for hop in hops:
            total = total + lax.ppermute(low, "fsdp", [(i, i ^ hop) for i in range(size)]).astype(jnp.float32)
    sketch = total.reshape(rank_in, examples, rank_out).transpose(1, 0, 2)
    sketch = sketch.reshape(examples, rank_in * rank_out)
    return score(sketch, queries_t, size)


def solution(mesh):
    order = ring_order(mesh.shape["fsdp"], folded=mesh.shape["parts"] == 2)

    def per_device(*args):
        return on_device(order, *args)

    return jax.shard_map(
        per_device,
        mesh=mesh,
        in_specs=(
            P(("parts", "dp"), None, "fsdp"),
            P(("parts", "dp"), None),
            P(None, "fsdp"),
            P(("parts", "dp"), None, "fsdp"),
            P(),
            P("fsdp", None),
            P("fsdp", "dp"),
        ),
        out_specs=(P(("parts", "dp"), "fsdp"), P(("parts", "dp"), "fsdp")),
        check_vma=False,
    )
```
